32 devices in a mesh: dp: 2 (over core), expert: 16 (over z, y, x).
Axes of the slice: x: 2, y: 2, z: 4, core: 2. Of those that a mesh axis runs over, the one named last changes fastest.
Arguments:
- tokens: bfloat16 [4096, 2048], P(('dp', 'expert')), may hold values from -6 to 6
- out_grad: bfloat16 [4096, 2048], P(('dp', 'expert')), may hold values from -6 to 6
- routes: int32 [4096, 8], P(('dp', 'expert')), may hold values from 0 to 15, all different within a row; in each aligned block of 128 rows (0 to 127, 128 to 255, ...) at most 128 rows name the same one
- probs: bfloat16 [4096, 8], P(('dp', 'expert')), may hold values from 0.019897461 to 1
- w_gate_up: bfloat16 [16, 2048, 768], P('expert'), may hold values from -0.125 to 0.125
- w_down: bfloat16 [16, 384, 2048], P('expert'), may hold values from -0.3125 to 0.3125
- moment_one: float32 [2, 16, 384, 2048], P('dp', 'expert'), may hold values from -12 to 12
- moment_two: float32 [2, 16, 384, 2048], P('dp', 'expert'), may hold values from 1 to 64
- replicas: int32 [16, 2], P('expert'), may hold values from 0 to 1, as said below
- leader: int32 [16], P('expert'), may hold values from 0 to 1
Outputs:
- token_grad: bfloat16 [4096, 2048], P(('dp', 'expert'))
- prob_grad: bfloat16 [4096, 8], P(('dp', 'expert'))
- new_down: bfloat16 [2, 16, 384, 2048], P('dp', 'expert')
- new_moment_one: float32 [2, 16, 384, 2048], P('dp', 'expert')
- new_moment_two: float32 [2, 16, 384, 2048], P('dp', 'expert')
The draws below stay inside these ranges and needn't reach their ends.
Inputs may be any that keep to these rules, and one draw needn't show every extreme that they name: `routes`: in the 128 rows of one device no expert is named by more than 128 rows. Each expert has one to 2 live replicas, its lead among them.
All inputs are finite; a program needn't handle non-finite values.
Results may differ from the reference program's by a relative error of at most 0.0064.
Values may be sent and summed in bfloat16 or wider, within the bound.
No kernel may reach another device: no remote copies, remote signals or barrier semaphores. Data moves between devices by JAX's collectives and lax.ppermute only.
A program may use at most 128 MiB of HBM per device.

```python
import math
import jax
import jax.numpy as jnp
import numpy as np
from jax import lax

D = 2048
FF_WIN = 384
TOP = 8
TOK_DEV = 128
EXPERTS = 16
TOKENS = 4096
CAP = 128
N_DP = 2
N_EXPERT = 16


def replica_sets(key):
    base = jax.random.fold_in(key, 7311)
    lead_key, keep_key = jax.random.split(base)
    leader = jax.random.randint(lead_key, (EXPERTS,), 0, N_DP).astype(jnp.int32)
    keeping = jax.random.randint(keep_key, (EXPERTS, N_DP), 0, 2).astype(jnp.int32)
    lead_hot = (jnp.arange(N_DP, dtype=jnp.int32)[None, :] == leader[:, None]).astype(jnp.int32)
    return (leader, jnp.maximum(keeping, lead_hot))


def draw_replicas(key, part):
    return replica_sets(key)[1]


def draw_leader(key, part):
    return replica_sets(key)[0]


def block_levels(stream_key, shape, pieces, smallest, top_value):
    def one(axis_at, blocks):
        draws = jax.random.uniform(jax.random.fold_in(jax.random.fold_in(stream_key, 6), axis_at), (blocks,), jnp.float32, smallest / len(pieces), top_value / len(pieces))
        return jnp.repeat(jnp.exp(draws), shape[axis_at] // blocks).reshape((-1,) + (1,) * (len(shape) - axis_at - 1))

    gain = one(*pieces[0])
    for cut in pieces[1:]:
        gain = gain * one(*cut)
    return gain


def deal_out(stream_key, own, number, rows, number_of, top, limit, lean):
    ranking = jax.random.permutation(stream_key, number_of)
    crowded, common = load_shares(number_of, rows * top, limit, lean, True), load_shares(number_of, rows * top, limit, lean, False)
    places = jnp.arange(number_of)

    def named(lengths, turn):
        used = int((lengths > 0).sum())
        fixed = max(1, used // 4)
        shifted = fixed + (places - fixed + turn * (used - fixed)) % max(1, number_of - fixed)
        return jnp.zeros((number_of,), jnp.int32).at[ranking[jnp.where(places < fixed, places, shifted)]].set(jnp.asarray(lengths, jnp.int32))

    lengths = jnp.where(number % 4 == 0, named(crowded, number // 4), named(common, number - number // 4 - 1))
    mixed = jax.random.permutation(jax.random.fold_in(own, 3), number_of)
    donor, sink = mixed[0:number_of // 2 * 2:2], mixed[1:number_of // 2 * 2:2]
    margin = jnp.minimum(lengths[donor] - 1, limit - lengths[sink]) // 2
    margin = jnp.where((donor == ranking[0]) | (sink == ranking[0]) | (lengths[sink] == 0), 0, jnp.maximum(margin, 0))
    shifted = jax.random.randint(jax.random.fold_in(own, 4), (number_of // 2,), 0, 1 << 20) % (margin + 1)
    lengths = lengths.at[donor].add(-shifted).at[sink].add(shifted)
    items = jnp.searchsorted(jnp.cumsum(lengths), jnp.arange(rows * top), side="right").astype(jnp.int32)
    grid = items.reshape(top, rows).T
    grid = grid[jax.random.permutation(jax.random.fold_in(own, 1), rows)]
    turn = jax.random.randint(jax.random.fold_in(own, 2), (rows, 1), 0, top)
    return jnp.take_along_axis(grid, (jnp.arange(top)[None, :] + turn) % top, axis=1)


def load_shares(amount, total, reach, lean, full):
    loads = [(1 << 20) // math.isqrt(grade ** lean) + 1 for grade in range(1, amount + 1)]
    largest = reach if full else min(reach, max(-(-total // amount), total * loads[0] // sum(loads)))
    least = 1 if total - largest >= amount - 1 else 0
    holding, rest = [largest] + [least] * (amount - 1), total - largest - least * (amount - 1)
    while rest > 0:
        movable = [i for i in range(1, amount) if holding[i] < largest] or [i for i in range(1, amount) if holding[i] < reach]
        whole, left = sum([loads[i] for i in movable]), rest
        for i in movable:
            extra = min(reach - holding[i], max(1, left * loads[i] // whole), rest)
            holding[i] = holding[i] + extra
            rest = rest - extra
    return np.array(holding)


def centred(own_key, shape, deviation, bound, shards=(), kind=jnp.bfloat16):
    drawn = jax.random.normal(own_key, shape, jnp.float32) * deviation
    if len(shards) > 0:
        drawn = block_levels(own_key, shape, shards, -0.22, 0.18) * drawn
    return jnp.clip(drawn, min=-bound, max=bound).astype(kind)


def setup_inputs(seed: int = 0) -> dict:
    key_of = jax.random.split(jax.random.key(seed), 11)
    tokens = centred(key_of[0], (TOKENS, D), 1.0, 6.0, ((0, 32),))
    out_grad = centred(key_of[1], (TOKENS, D), 1.0, 6.0, ((0, 32),))
    routes_keys = jax.random.split(jax.random.fold_in(key_of[2], 1), TOKENS // TOK_DEV)
    routes_turns = jax.random.permutation(jax.random.fold_in(key_of[2], 3), TOKENS // TOK_DEV)
    routes = jax.vmap(lambda own, number: deal_out(jax.random.fold_in(key_of[2], 2), own, number, TOK_DEV, EXPERTS, TOP, CAP, 2))(routes_keys, routes_turns).reshape((TOKENS, TOP))
    probs = jnp.clip(jnp.exp(math.log(1.0) - 3.9171631 * jax.random.uniform(key_of[3], (TOKENS, TOP), jnp.float32) ** block_levels(key_of[3], (TOKENS, TOP), ((0, 32),), -0.2, 0.2)), 0.019897461, 1.0).astype(jnp.bfloat16)
    w_gate_up = centred(key_of[4], (EXPERTS, D, 2 * FF_WIN), D ** -0.5, 0.125, ((0, 16),))
    w_down = centred(key_of[5], (EXPERTS, FF_WIN, D), FF_WIN ** -0.5, 0.3125, ((0, 16),))
    moment_one = centred(key_of[6], (N_DP, EXPERTS, FF_WIN, D), 2.0, 12.0, ((0, 2), (1, 16)), jnp.float32)
    moment_two = jnp.clip(jnp.exp(math.log(64.0) - 4.158883 * jax.random.uniform(key_of[7], (N_DP, EXPERTS, FF_WIN, D), jnp.float32) ** block_levels(key_of[7], (N_DP, EXPERTS, FF_WIN, D), ((0, 2), (1, 16)), -0.2, 0.2)), 1.0, 64.0)
    replicas = draw_replicas(jax.random.fold_in(key_of[10], 71), 0)
    leader = draw_leader(jax.random.fold_in(key_of[10], 71), 0)
    return dict(tokens=tokens, out_grad=out_grad, routes=routes, probs=probs, w_gate_up=w_gate_up, w_down=w_down, moment_one=moment_one, moment_two=moment_two, replicas=replicas, leader=leader)


learn_rate = 0.01
beta_one = 0.9
beta_two = 0.95
adam_eps = 1e-08
weight_decay = 0.1
adam_step = 100

def expert_rows(gate_up, grads, weights, w_gu, w_dn):
    half = w_dn.shape[0]
    gate = gate_up[:, :half]
    upper = gate_up[:, half:]
    sigma = jax.nn.sigmoid(gate)
    silu_val = gate * sigma
    hidden = (silu_val * upper).astype(jnp.bfloat16)
    grads_wide = grads.astype(jnp.float32)
    scaled = (weights.astype(jnp.float32)[:, None] * grads_wide).astype(jnp.bfloat16)
    output = jnp.dot(hidden, w_dn, preferred_element_type=jnp.float32)
    pair_prob = lax.optimization_barrier(jnp.sum(grads_wide * output, axis=1)).astype(jnp.bfloat16)
    hidden_grad = lax.dot_general(scaled, w_dn, (((1,), (1,)), ((), ())), preferred_element_type=jnp.float32)
    deriv = sigma * (1.0 + gate * (1.0 - sigma))
    pre_grad = jnp.concatenate([hidden_grad * upper * deriv, hidden_grad * silu_val], axis=1).astype(jnp.bfloat16)
    pair_grad = lax.dot_general(pre_grad, w_gu, (((1,), (1,)), ((), ())), preferred_element_type=jnp.float32).astype(jnp.bfloat16)
    weight_grad = lax.dot_general(hidden, scaled, (((0,), (0,)), ((), ())), preferred_element_type=jnp.float32)
    return (pair_grad, pair_prob, weight_grad)

def adam_update(grad, m_old, v_old, w_old):
    m_new = beta_one * m_old + (1.0 - beta_one) * grad
    v_new = beta_two * v_old + (1.0 - beta_two) * grad * grad
    m_hat = m_new / (1.0 - beta_one ** adam_step)
    v_hat = v_new / (1.0 - beta_two ** adam_step)
    w_wide = w_old.astype(jnp.float32)
    w_new = (w_wide - learn_rate * (m_hat / (jnp.sqrt(v_hat) + adam_eps) + weight_decay * w_wide)).astype(jnp.bfloat16)
    return (m_new, v_new, w_new)

def reference(tokens, out_grad, routes, probs, w_gate_up, w_down, moment_one, moment_two, replicas, leader):
    assign_count = TOKENS * TOP
    most_rows = N_DP * N_EXPERT * CAP
    flat = routes.reshape(-1).astype(jnp.int32)
    flat_probs = probs.reshape(-1)
    padded_tokens = jnp.concatenate([tokens, jnp.zeros((1, D), jnp.bfloat16)], axis=0)
    padded_grads = jnp.concatenate([out_grad, jnp.zeros((1, D), jnp.bfloat16)], axis=0)

    def per_expert(carry, expert_id):
        token_acc, prob_acc = carry
        picks = jnp.nonzero(flat == expert_id, size=most_rows, fill_value=assign_count)[0].astype(jnp.int32)
        valid = picks < assign_count
        token_of = jnp.where(valid, picks // TOP, TOKENS).astype(jnp.int32)
        inputs = padded_tokens[token_of]
        grads = padded_grads[token_of]
        safe = jnp.minimum(picks, assign_count - 1).astype(jnp.int32)
        weights = jnp.where(valid, flat_probs[safe], jnp.zeros((), jnp.bfloat16))
        gate_up = jnp.dot(inputs, w_gate_up[expert_id], preferred_element_type=jnp.float32)
        pair_grad, pair_prob, weight_grad = expert_rows(gate_up, grads, weights, w_gate_up[expert_id], w_down[expert_id])
        token_acc = token_acc.at[token_of].add(pair_grad.astype(jnp.float32), mode='drop')
        prob_acc = prob_acc.at[picks].set(pair_prob, mode='drop')
        return ((token_acc, prob_acc), weight_grad)
    start = (jnp.zeros((TOKENS, D), jnp.float32), jnp.zeros((assign_count,), jnp.bfloat16))
    (token_acc, prob_acc), grad_down = lax.scan(per_expert, start, jnp.arange(EXPERTS, dtype=jnp.int32))
    token_grad = token_acc.astype(jnp.bfloat16)
    prob_grad = prob_acc.reshape(TOKENS, TOP)
    expert_ids = jnp.arange(EXPERTS, dtype=jnp.int32)
    lead_m = moment_one[leader, expert_ids]
    lead_v = moment_two[leader, expert_ids]
    m_new, v_new, w_new = adam_update(grad_down, lead_m, lead_v, w_down)
    is_lead = (jnp.arange(N_DP, dtype=jnp.int32)[:, None] == leader[None, :])[:, :, None, None]
    live = (jnp.transpose(replicas) == 1)[:, :, None, None]
    new_down = jnp.where(live, w_new[None], w_down[None])
    new_moment_one = jnp.where(is_lead, m_new[None], moment_one)
    new_moment_two = jnp.where(is_lead, v_new[None], moment_two)
    return (token_grad, prob_grad, new_down, new_moment_one, new_moment_two)
```

```python
import jax
import jax.numpy as jnp
from jax import lax
from jax.sharding import PartitionSpec as P

learn_rate = 0.01
beta_one = 0.9
beta_two = 0.95
adam_eps = 1e-08
weight_decay = 0.1
adam_step = 100

f32 = jnp.float32
bf16 = jnp.bfloat16


def adam_update(grad, m_old, v_old, w_old):
    m_new = beta_one * m_old + (1.0 - beta_one) * grad
    v_new = beta_two * v_old + (1.0 - beta_two) * grad * grad
    m_hat = m_new / (1.0 - beta_one**adam_step)
    v_hat = v_new / (1.0 - beta_two**adam_step)
    w_wide = w_old.astype(f32)
    w_new = (
        w_wide - learn_rate * (m_hat / (jnp.sqrt(v_hat) + adam_eps) + weight_decay * w_wide)
    ).astype(bf16)
    return (m_new, v_new, w_new)


def hop(value, flip):
    n = lax.axis_size("expert")
    return lax.ppermute(value, "expert", [(i, i ^ flip) for i in range(n)])


def turn(value, step):
    n = lax.axis_size("dp")
    return lax.ppermute(value, "dp", [((r + step) % n, r) for r in range(n)])


def nt(a, b):
    return lax.dot_general(a, b, (((1,), (1,)), ((), ())), preferred_element_type=f32)


def tn(a, b):
    return lax.dot_general(a, b, (((0,), (0,)), ((), ())), preferred_element_type=f32)


def body(
    tokens, out_grad, routes, probs, w_gate_up, w_down, moment_one, moment_two, replicas, leader
):
    tok_dev, model = tokens.shape
    half = w_down.shape[1]
    n_dp = lax.axis_size("dp")
    n_ex = lax.axis_size("expert")
    plane = 4
    layers = n_ex // plane
    width = model // n_dp
    me_dp = lax.axis_index("dp")
    me = lax.axis_index("expert")
    here = me % plane
    layer = me // plane

    def roll(value, axis):
        both = jnp.concatenate([value, value], axis)
        return lax.dynamic_slice_in_dim(both, me_dp * width, model, axis)

    def unroll(value, axis):
        both = jnp.concatenate([value, value], axis)
        return lax.dynamic_slice_in_dim(both, (n_dp - me_dp) % n_dp * width, model, axis)

    gu_own = roll(w_gate_up[0], 0)
    dn_own = roll(w_down[0], 1)
    gu_0 = gu_own[:width]
    dn_0 = dn_own[:, :width]
    gu_1 = hop(gu_0, 1)
    dn_2 = hop(dn_0, 2)
    dn_1 = hop(dn_0, 1)
    gu_2 = hop(gu_0, 2)
    gu_3 = hop(gu_1, 2)
    dn_3 = hop(dn_2, 1)

    def parts(value):
        return [value] + [turn(value, k) for k in range(1, n_dp)]

    gus = [[gu_own[k * width : (k + 1) * width] for k in range(n_dp)]]
    dns = [[dn_own[:, k * width : (k + 1) * width] for k in range(n_dp)]]
    for gu, dn in ((gu_1, dn_1), (gu_2, dn_2), (gu_3, dn_3)):
        gus.append(parts(gu))
        dns.append(parts(dn))

    x_own = roll(tokens, 1)
    y_own = roll(out_grad, 1)
    rows_x = jnp.concatenate([x_own] + [hop(x_own, plane * k) for k in range(1, layers)], 0)
    rows_y = jnp.concatenate([y_own] + [hop(y_own, plane * k) for k in range(1, layers)], 0)

    def expert_of(k, s):
        return (layer ^ k) * plane + (here ^ s)

    wide = probs.astype(f32)
    named = [
        [
            jnp.sum(jnp.where(routes == expert_of(k, s), wide, 0.0), axis=1, keepdims=True)
            for s in range(plane)
        ]
        for k in range(layers)
    ]
    p_rows = jnp.concatenate(
        [
            jnp.concatenate(named[0], 1),
            *[
                hop(jnp.concatenate(named[k], 1).astype(bf16), plane * k).astype(f32)
                for k in range(1, layers)
            ],
        ],
        0,
    )

    x_parts = [rows_x[:, k * width : (k + 1) * width] for k in range(n_dp)]
    y_parts = [rows_y[:, k * width : (k + 1) * width] for k in range(n_dp)]
    dx = [0.0] * n_dp
    pair_probs = []
    grads = []
    for s in range(plane):
        gate_up = sum(
            jnp.dot(x_parts[k], gus[s][k], preferred_element_type=f32) for k in range(n_dp)
        )
        back = sum(nt(y_parts[k], dns[s][k]) for k in range(n_dp))
        p = p_rows[:, s : s + 1]
        gate, upper = gate_up[:, :half], gate_up[:, half:]
        sigma = jax.nn.sigmoid(gate)
        silu = gate * sigma
        hidden = (silu * upper).astype(bf16).astype(f32)
        pair_probs.append(jnp.sum(hidden * back, axis=1, keepdims=True))
        hidden_grad = p * back
        deriv = sigma * (1.0 + gate * (1.0 - sigma))
        pre_grad = jnp.concatenate(
            [hidden_grad * upper * deriv, hidden_grad * silu], axis=1
        ).astype(bf16)
        scaled = (p * hidden).astype(bf16)
        dx = [dx[k] + nt(pre_grad, gus[s][k]) for k in range(n_dp)]
        mine = [tn(scaled, y_parts[k]) for k in range(n_dp)]
        mine = mine[0] + sum(turn(mine[n_dp - k], k) for k in range(1, n_dp))
        grads.append(mine)

    dx = jnp.concatenate(dx, 1).reshape(layers, tok_dev, model)
    total = dx[0] + sum(
        hop(dx[k].astype(bf16), plane * k).astype(f32) for k in range(1, layers)
    )
    token_grad = unroll(total.astype(bf16), 1)
    pair_prob = jnp.concatenate(pair_probs, 1).reshape(layers, tok_dev, plane).astype(bf16)
    pair_prob = [pair_prob[0]] + [hop(pair_prob[k], plane * k) for k in range(1, layers)]
    prob_grad = sum(
        jnp.where(routes == expert_of(k, s), pair_prob[k][:, s : s + 1].astype(f32), 0.0)
        for k in range(layers)
        for s in range(plane)
    ).astype(bf16)

    grad = grads[0] + sum(hop(grads[s].astype(bf16), s).astype(f32) for s in range(1, plane))
    grad = unroll(jnp.concatenate(parts(grad), 1), 1)
    m_old, v_old, w_old = moment_one[0, 0], moment_two[0, 0], w_down[0]
    m_new, v_new, w_new = adam_update(grad, m_old, v_old, w_old)
    lead = leader[0]
    fresh = w_new
    for k in range(1, n_dp):
        fresh = jnp.where((me_dp + k) % n_dp == lead, turn(w_new, k), fresh)
    is_lead = me_dp == lead
    is_live = replicas[0][me_dp] == 1
    new_down = jnp.where(is_live, fresh, w_old)[None, None]
    new_one = jnp.where(is_lead, m_new, m_old)[None, None]
    new_two = jnp.where(is_lead, v_new, v_old)[None, None]
    return (token_grad, prob_grad, new_down, new_one, new_two)


def solution(mesh):
    in_specs = (
        P(("dp", "expert"), None),
        P(("dp", "expert"), None),
        P(("dp", "expert"), None),
        P(("dp", "expert"), None),
        P("expert", None, None),
        P("expert", None, None),
        P("dp", "expert", None, None),
        P("dp", "expert", None, None),
        P("expert", None),
        P("expert"),
    )
    out_specs = (
        P(("dp", "expert"), None),
        P(("dp", "expert"), None),
        P("dp", "expert", None, None),
        P("dp", "expert", None, None),
        P("dp", "expert", None, None),
    )
    return jax.shard_map(body, mesh=mesh, in_specs=in_specs, out_specs=out_specs, check_vma=False)
```

```python
import functools
import jax
import jax.numpy as jnp
from jax import lax
from jax.experimental import pallas as pl
from jax.experimental.pallas import tpu as pltpu
from jax.sharding import PartitionSpec as P

learn_rate = 0.01
beta_one = 0.9
beta_two = 0.95
adam_eps = 1e-08
weight_decay = 0.1
adam_step = 100

f32 = jnp.float32
bf16 = jnp.bfloat16
plane = 4
lanes = 128
tile = 256


def adam_update(grad, m_old, v_old, w_old):
    m_new = beta_one * m_old + (1.0 - beta_one) * grad
    v_new = beta_two * v_old + (1.0 - beta_two) * grad * grad
    m_hat = m_new / (1.0 - beta_one**adam_step)
    v_hat = v_new / (1.0 - beta_two**adam_step)
    w_wide = w_old.astype(f32)
    w_new = (
        w_wide - learn_rate * (m_hat / (jnp.sqrt(v_hat) + adam_eps) + weight_decay * w_wide)
    ).astype(bf16)
    return (m_new, v_new, w_new)


def hop(value, flip):
    n = lax.axis_size("expert")
    return lax.ppermute(value, "expert", [(i, i ^ flip) for i in range(n)])


def climb(value, way, low, high):
    pairs = [(i, i + way * plane) for i in range(low * plane, high * plane)]
    return lax.ppermute(value, "expert", pairs)


def turn(value, step):
    n = lax.axis_size("dp")
    return lax.ppermute(value, "dp", [((r + step) % n, r) for r in range(n)])


def after(value, *earlier):
    return lax.optimization_barrier((value, *earlier))[0]


def nt(a, b):
    return lax.dot_general(a, b, (((1,), (1,)), ((), ())), preferred_element_type=f32)


def tn(a, b):
    return lax.dot_general(a, b, (((0,), (0,)), ((), ())), preferred_element_type=f32)


def source(layer, k):
    far = layer ^ k
    return ("down", far - layer) if far > layer else ("up", layer - far)


class Pass:
    def __init__(self, tok, model, half, n_ex, n_dp, slots, blocks, last):
        self.tok, self.model, self.half, self.n_ex, self.n_dp = tok, model, half, n_ex, n_dp
        self.slots, self.blocks, self.last = slots, blocks, last
        self.layers = n_ex // plane
        self.rows = tok * len(blocks)
        self.width = model // n_dp
        self.tail = -(-n_ex // 16) * 16

    def kernel(self, n_in, *refs):
        tok, model, half, rows, width = self.tok, self.model, self.half, self.rows, self.width
        n_dp, layers, slots, blocks = self.n_dp, self.layers, self.slots, self.blocks
        ins = dict(zip(self.names, refs[:n_in]))
        n_out = len(self.outs)
        outs = dict(zip(self.outs, refs[n_in : n_in + n_out]))
        scratch = list(refs[n_in + n_out :])
        xs, ys, ps, ws, gu, back, pre, sc, pcol, dx, pr, keep, send = scratch[:13]
        sem_t, sem_w, sem_i, sem_o = scratch[13:17]
        me_dp = lax.axis_index("dp")
        me = lax.axis_index("expert")
        here, layer = lax.rem(me, plane), lax.div(me, plane)

        def row_copies(ref, b):
            at = pl.ds(b * tok, tok)
            return (
                pltpu.make_async_copy(ref.at[pl.ds(0, tok)], xs.at[at], sem_t.at[b, 0]),
                pltpu.make_async_copy(ref.at[pl.ds(tok, tok)], ys.at[at], sem_t.at[b, 1]),
                pltpu.make_async_copy(
                    ref.at[pl.ds(2 * tok, self.tail), pl.ds(0, lanes)],
                    ps.at[b, pl.ds(0, self.tail)],
                    sem_t.at[b, 2],
                ),
            )

        ps[...] = jnp.zeros_like(ps)
        for b, k in enumerate(blocks):
            if k == 0:
                for copy in row_copies(ins["own"], b):
                    copy.start()
                continue
            for z in range(layers):

                @pl.when(layer == z)
                def _(b=b, k=k, z=z):
                    for copy in row_copies(ins[source(z, k)], b):
                        copy.start()

        def weight_copies(i):
            s = slots[i]
            if s == 0:
                return [pltpu.make_async_copy(ins["w0"], ws.at[i % 2], sem_w.at[i, 0])]
            out = []
            for k in range(n_dp):
                for h in range(2):
                    at = lax.rem(me_dp + k, n_dp) * width + h * (width // 2)
                    at = pl.multiple_of(at, width // 2)
                    out.append(
                        pltpu.make_async_copy(
                            ins["w%d_%d_%d" % (s, k, h)],
                            ws.at[i % 2, pl.ds(at, width // 2)],
                            sem_w.at[i, 2 * k + h],
                        )
                    )
            return out

        for copy in weight_copies(0):
            copy.start()
        extra = []
        held = {"dx": 0, "pr": 0, "keep": 0, "send": 0}
        for name, ref in ins.items():
            kind = name[0][:-1] if isinstance(name, tuple) and name[0][:-1] in held else None
            if kind is None:
                continue
            n = ref.shape[0]
            to = {"dx": dx, "pr": pr, "keep": keep, "send": send}[kind].at[pl.ds(held[kind], n)]
            extra.append(pltpu.make_async_copy(ref, to, sem_i.at[len(extra)]))
            held[kind] += n
        if not held["pr"]:
            pr[...] = jnp.zeros_like(pr)
        for copy in extra:
            copy.start()

        for b in range(len(blocks)):
            for copy in row_copies(ins["own"], b):
                copy.wait()
            pcol[pl.ds(b * tok, tok), :] = jnp.transpose(ps[b].astype(f32))
        chunk = min(128, tok)
        lane = lax.broadcasted_iota(jnp.int32, (chunk, lanes), 1)
        pending = []

        for i, s in enumerate(slots):
            for copy in weight_copies(i):
                copy.wait()
            if i + 1 < len(slots):
                for copy in weight_copies(i + 1):
                    copy.start()
            w = ws.at[i % 2]
            for n in range(0, 2 * half, tile):
                gu[:, n : n + tile] = jnp.dot(
                    xs[...], w[:, n : n + tile], preferred_element_type=f32
                )
            back[...] = jnp.dot(ys[...], w[:, 2 * half :], preferred_element_type=f32)
            if i == 0:
                for copy in extra:
                    copy.wait()
            expert = layer * plane + lax.bitwise_xor(here, jnp.int32(s))

            @pl.loop(0, rows // chunk)
            def _(r):
                at = pl.ds(pl.multiple_of(r * chunk, chunk), chunk)
                gate, upper, h = gu[at, :half], gu[at, half:], back[at, :]
                hit = lane == expert
                p = jnp.sum(jnp.where(hit, pcol[at, :], 0.0), axis=1, keepdims=True)
                sigma = jax.nn.sigmoid(gate)
                silu = gate * sigma
                hidden = (silu * upper).astype(bf16).astype(f32)
                pair = jnp.sum(hidden * h, axis=1, keepdims=True)
                pr[at, :] += jnp.where(hit, pair, 0.0)
                grad = p * h
                pre[at, :half] = (grad * upper * (sigma * (1.0 + gate * (1.0 - sigma)))).astype(bf16)
                pre[at, half:] = (grad * silu).astype(bf16)
                sc[at, :] = (p * hidden).astype(bf16)

            add_dx = held["dx"] or i > 0
            for d in range(0, model, 2 * tile):
                at = slice(d, d + 2 * tile)
                part = nt(pre[...], w[at, : 2 * half])
                dx[:, at] = dx[:, at] + part if add_dx else part
            for d in range(0, width, 2 * tile):
                at = slice(d, d + 2 * tile)
                col = pl.ds(pl.multiple_of(me_dp * width + d, tile), 2 * tile)
                part = tn(sc[...], ys[:, col])
                keep[i, :, at] = keep[i, :, at] + part if held["keep"] else part
                for k in range(1, n_dp):
                    col = lax.rem(me_dp + n_dp - k, n_dp) * width + d
                    part = tn(sc[...], ys[:, pl.ds(pl.multiple_of(col, tile), 2 * tile)])
                    if held["send"]:
                        part = send[i, k - 1, :, at].astype(f32) + part
                    send[i, k - 1, :, at] = part.astype(bf16)

            pending.append(
                pltpu.make_async_copy(keep.at[i], outs["keep"].at[i], sem_o.at[2 * i])
            )
            pending.append(
                pltpu.make_async_copy(send.at[i], outs["send"].at[i], sem_o.at[2 * i + 1])
            )
            pending[-2].start()
            pending[-1].start()
        n = 2 * len(slots)
        if not self.last:
            pending.append(pltpu.make_async_copy(dx, outs["dx"], sem_o.at[n]))
            pending.append(pltpu.make_async_copy(pr, outs["pr"], sem_o.at[n + 1]))
            pending[-2].start()
            pending[-1].start()
        else:
            rows_out = scratch[17]
            for b, k in enumerate(blocks):
                at = pl.ds(b * tok, tok)
                rows_out[b, pl.ds(0, tok), :] = dx[at, :].astype(bf16)
                rows_out[b, pl.ds(tok, self.tail), :] = jnp.zeros((self.tail, model), bf16)
                turned = jnp.transpose(pr[at, :])[: self.tail]
                rows_out[b, pl.ds(tok, self.tail), pl.ds(0, lanes)] = turned.astype(bf16)
                dest = lax.bitwise_xor(layer, jnp.int32(k))
                copy = pltpu.make_async_copy(rows_out.at[b], outs["back"].at[dest], sem_o.at[n + b])
                copy.start()
                pending.append(copy)
        for copy in pending:
            copy.wait()

    def call(self, ins):
        tok, model, half, rows, width = self.tok, self.model, self.half, self.rows, self.width
        n_dp, n = self.n_dp, len(self.slots)
        shape = {"keep": ((n, half, width), f32)}
        shape["send"] = ((n, max(n_dp - 1, 1), half, width), bf16)
        if self.last:
            shape["back"] = ((self.layers, tok + self.tail, model), bf16)
        else:
            shape["dx"] = ((rows, model), f32)
            shape["pr"] = ((rows, lanes), f32)
        self.names, self.outs = list(ins), list(shape)
        scratch = [
            pltpu.VMEM((rows, model), bf16),
            pltpu.VMEM((rows, model), bf16),
            pltpu.VMEM((len(self.blocks), tok, lanes), bf16),
            pltpu.VMEM((min(n, 2), model, 3 * half), bf16),
            pltpu.VMEM((rows, 2 * half), f32),
            pltpu.VMEM((rows, half), f32),
            pltpu.VMEM((rows, 2 * half), bf16),
            pltpu.VMEM((rows, half), bf16),
            pltpu.VMEM((rows, lanes), f32),
            pltpu.VMEM((rows, model), f32),
            pltpu.VMEM((rows, lanes), f32),
            pltpu.VMEM((n, half, width), f32),
            pltpu.VMEM((n, max(n_dp - 1, 1), half, width), bf16),
            pltpu.SemaphoreType.DMA((len(self.blocks), 3)),
            pltpu.SemaphoreType.DMA((n, 2 * n_dp)),
            pltpu.SemaphoreType.DMA((8,)),
            pltpu.SemaphoreType.DMA((2 * n + len(self.blocks) + 2,)),
        ]
        if self.last:
            scratch.append(pltpu.VMEM((self.layers, tok + self.tail, model), bf16))
        out = pl.pallas_call(
            functools.partial(self.kernel, len(ins)),
            out_shape=[jax.ShapeDtypeStruct(*v) for v in shape.values()],
            in_specs=[pl.BlockSpec(memory_space=pl.ANY)] * len(ins),
            out_specs=[pl.BlockSpec(memory_space=pl.ANY)] * len(shape),
            scratch_shapes=scratch,
            compiler_params=pltpu.CompilerParams(vmem_limit_bytes=56 * 2**20),
            cost_estimate=pl.CostEstimate(flops=1000, bytes_accessed=1000, transcendentals=0),
        )(*ins.values())
        return dict(zip(shape, out))


def adam_kernel(n_dp, lead_ref, *refs):
    grads = refs[:n_dp]
    m_ref, v_ref, w_ref, m_out, v_out, w_out = refs[n_dp:]
    me_dp = lax.axis_index("dp")
    width = grads[0].shape[1]
    is_lead = lead_ref[0] == me_dp
    for k, ref in enumerate(grads):
        at = lax.rem(me_dp + k, n_dp) * width
        at = pl.ds(pl.multiple_of(at, width), width)
        m_old, v_old = m_ref[0, 0, :, at], v_ref[0, 0, :, at]
        m_new, v_new, w_new = adam_update(ref[...].astype(f32), m_old, v_old, w_ref[0, :, at])
        m_out[0, 0, :, at] = jnp.where(is_lead, m_new, m_old)
        v_out[0, 0, :, at] = jnp.where(is_lead, v_new, v_old)
        w_out[:, at] = w_new


def adam_call(parts, leader, moment_one, moment_two, w_down):
    half, model = w_down.shape[1:]
    step = 48 if half % 48 == 0 else half
    n_dp = len(parts)
    width = model // n_dp
    wide = pl.BlockSpec((1, 1, step, model), lambda i: (0, 0, i, 0))
    return pl.pallas_call(
        functools.partial(adam_kernel, n_dp),
        grid=(half // step,),
        out_shape=[
            jax.ShapeDtypeStruct(moment_one.shape, f32),
            jax.ShapeDtypeStruct(moment_two.shape, f32),
            jax.ShapeDtypeStruct((half, model), bf16),
        ],
        in_specs=[pl.BlockSpec(memory_space=pltpu.SMEM)]
        + [pl.BlockSpec((step, width), lambda i: (i, 0))] * n_dp
        + [wide, wide, pl.BlockSpec((1, step, model), lambda i: (0, i, 0))],
        out_specs=[wide, wide, pl.BlockSpec((step, model), lambda i: (i, 0))],
        compiler_params=pltpu.CompilerParams(vmem_limit_bytes=32 * 2**20),
        cost_estimate=pl.CostEstimate(
            flops=20 * half * model, bytes_accessed=20 * half * model, transcendentals=0
        ),
    )(leader, *parts, moment_one, moment_two, w_down)


def body(
    tokens, out_grad, routes, probs, w_gate_up, w_down, moment_one, moment_two, replicas, leader
):
    tok_dev, model = tokens.shape
    half = w_down.shape[1]
    n_dp = lax.axis_size("dp")
    n_ex = lax.axis_size("expert")
    layers = n_ex // plane
    width = model // n_dp
    me_dp = lax.axis_index("dp")
    me = lax.axis_index("expert")
    layer = me // plane
    tail = -(-n_ex // 16) * 16

    def others(value):
        return [turn(value, k) for k in range(1, n_dp)]

    wide = probs.astype(f32)
    ids = jnp.arange(tail, dtype=jnp.int32)
    chosen = routes.T[None] == ids[:, None, None]
    p_all = jnp.sum(jnp.where(chosen, wide.T[None], 0.0), axis=1).astype(bf16)
    p_all = jnp.pad(p_all, ((0, 0), (0, model - tok_dev)))
    own = jnp.concatenate([tokens, out_grad, p_all], 0)
    w_gu, w_dn = w_gate_up[0], w_down[0]
    w_own = jnp.concatenate([w_gu, w_dn.T], 1)
    p1 = lax.dynamic_slice_in_dim(w_own, me_dp * width, width // 2, 0)
    p2 = lax.dynamic_slice_in_dim(w_own, me_dp * width + width // 2, width // 2, 0)
    up, down = {}, {}
    up[1], down[1] = climb(own, 1, 0, layers - 1), climb(own, -1, 1, layers)
    x_p1, y_p2 = hop(p1, 1), hop(p2, 2)

    p1, p2, up[1], down[1], x_p1, y_p2 = lax.optimization_barrier(
        (p1, p2, up[1], down[1], x_p1, y_p2)
    )
    x_p2, y_p1 = hop(p2, 1), hop(p1, 2)
    if layers > 2:
        up[2], down[2] = climb(up[1], 1, 1, layers - 1), climb(down[1], -1, 1, layers - 1)
    x_o1 = others(x_p1)
    y_o2 = others(after(y_p2, *x_o1))

    (x_p1, y_p2, x_p2, y_p1, x_o1, y_o2, up, down) = lax.optimization_barrier(
        (x_p1, y_p2, x_p2, y_p1, x_o1, y_o2, up, down)
    )
    d_p2, d_p1 = hop(y_p2, 1), hop(x_p1, 2)
    for k in range(3, layers):
        up[k] = climb(up[k - 1], 1, k - 1, layers - 1)
        down[k] = climb(down[k - 1], -1, 1, layers - k + 1)
    x_o2 = others(x_p2)
    y_o1 = others(after(y_p1, *x_o2))
    weights = {"w0": w_own}

    def name_parts(s, firsts, seconds):
        for k in range(n_dp):
            weights["w%d_%d_0" % (s, k)] = firsts[k]
            weights["w%d_%d_1" % (s, k)] = seconds[k]

    name_parts(1, [x_p1] + x_o1, [x_p2] + x_o2)
    name_parts(2, [y_p1] + y_o1, [y_p2] + y_o2)

    def pick(slots, blocks):
        got = {"own": own}
        for k in blocks:
            for z in range(layers):
                if k:
                    way, steps = source(z, k)
                    got[(way, steps)] = (up if way == "up" else down)[steps]
        for name, value in weights.items():
            if int(name[1]) in slots:
                got[name] = value
        return got

    near, far = list(range(layers - 1)), [layers - 1]
    make = functools.partial(Pass, tok_dev, model, half, n_ex, n_dp)

    def carry(*passes):
        return {(k + str(i), i): p[k] for i, (p, keys) in enumerate(passes) for k in keys}

    zero = make([0], near, False).call(pick([0], near))
    one = make([1, 2], near, False).call(pick([1, 2], near) | carry((zero, ("dx", "pr"))))

    zero, one, d_p1, d_p2, up, down = lax.optimization_barrier((zero, one, d_p1, d_p2, up, down))
    d_o1 = others(d_p1)
    d_o2 = others(after(d_p2, *d_o1))
    name_parts(3, [d_p1] + d_o1, [d_p2] + d_o2)
    grads = ("keep", "send")
    two = make([0, 1, 2], far, False).call(pick([0, 1, 2], far) | carry((zero, grads), (one, grads)))
    last = make([3], near + far, True).call(
        pick([3], near + far) | carry((one, ("dx", "pr")), (two, ("dx", "pr")))
    )

    swapped = [turn(two["send"][:, k - 1], k) for k in range(1, n_dp)]
    sent = [
        hop((two["keep"][s] + sum(v[s].astype(f32) for v in swapped)).astype(bf16), s)
        for s in (1, 2)
    ]
    swapped_across = [turn(last["send"][0, k - 1], k) for k in range(1, n_dp)]
    across = last["keep"][0] + sum(v.astype(f32) for v in swapped_across)
    sent.append(hop(across.astype(bf16), 3))
    back = last["back"]

    def term(dest):
        return lax.dynamic_index_in_dim(back, dest, 0, False).astype(f32)

    from_below = from_above = 0.0
    for k in range(layers - 1, 0, -1):
        send_up = (term(jnp.minimum(layer + k, layers - 1)) + from_below).astype(bf16)
        send_down = (term(jnp.maximum(layer - k, 0)) + from_above).astype(bf16)
        send_up, send_down = lax.optimization_barrier((send_up, send_down))
        from_below = climb(send_up, 1, 0, layers - k)
        from_above = climb(send_down, -1, k, layers)
        if k > 1:
            from_below, from_above = from_below.astype(f32), from_above.astype(f32)

    sent = lax.optimization_barrier((sent, send_up, send_down))[0]
    grad = two["keep"][0] + sum(v[0].astype(f32) for v in swapped)
    grad = (grad + sum(v.astype(f32) for v in sent)).astype(bf16)
    parts = [grad] + others(grad)
    new_one, new_two, w_new = adam_call(parts, leader, moment_one, moment_two, w_down)
    lead = leader[0]
    fresh = w_new
    for k in range(1, n_dp):
        fresh = jnp.where((me_dp + k) % n_dp == lead, turn(w_new, k), fresh)

    from_below, from_above = lax.optimization_barrier((from_below, from_above, w_new))[:2]
    total = term(layer) + from_below.astype(f32) + from_above.astype(f32)
    token_grad = total[:tok_dev].astype(bf16)
    pair = total[tok_dev:, :tok_dev]
    prob_grad = jnp.sum(jnp.where(chosen, pair[:, None, :], 0.0), axis=0).T.astype(bf16)
    is_live = replicas[0][me_dp] == 1
    new_down = jnp.where(is_live, fresh, w_dn)[None, None]
    return (token_grad, prob_grad, new_down, new_one, new_two)


def solution(mesh):
    in_specs = (
        P(("dp", "expert"), None),
        P(("dp", "expert"), None),
        P(("dp", "expert"), None),
        P(("dp", "expert"), None),
        P("expert", None, None),
        P("expert", None, None),
        P("dp", "expert", None, None),
        P("dp", "expert", None, None),
        P("expert", None),
        P("expert"),
    )
    out_specs = (
        P(("dp", "expert"), None),
        P(("dp", "expert"), None),
        P("dp", "expert", None, None),
        P("dp", "expert", None, None),
        P("dp", "expert", None, None),
    )
    return jax.shard_map(body, mesh=mesh, in_specs=in_specs, out_specs=out_specs, check_vma=False)
```

```python
import functools
import jax
import jax.numpy as jnp
from jax import lax
from jax.experimental import pallas as pl
from jax.experimental.pallas import tpu as pltpu
from jax.sharding import PartitionSpec as P

learn_rate = 0.01
beta_one = 0.9
beta_two = 0.95
adam_eps = 1e-08
weight_decay = 0.1
adam_step = 100

f32 = jnp.float32
bf16 = jnp.bfloat16
plane = 4
lanes = 128
tile = 256


def adam_update(grad, m_old, v_old, w_old):
    m_new = beta_one * m_old + (1.0 - beta_one) * grad
    v_new = beta_two * v_old + (1.0 - beta_two) * grad * grad
    m_hat = m_new / (1.0 - beta_one**adam_step)
    v_hat = v_new / (1.0 - beta_two**adam_step)
    w_wide = w_old.astype(f32)
    w_new = (
        w_wide - learn_rate * (m_hat / (jnp.sqrt(v_hat) + adam_eps) + weight_decay * w_wide)
    ).astype(bf16)
    return (m_new, v_new, w_new)


def hop(value, flip):
    n = lax.axis_size("expert")
    return lax.ppermute(value, "expert", [(i, i ^ flip) for i in range(n)])


def ring(layers):
    return [z for z in range(layers) if z == 0 or z % 2] + [
        z for z in range(layers - 1, 0, -1) if z % 2 == 0
    ]


def along(value):
    n = lax.axis_size("expert")
    order = ring(n // plane)
    pairs = [
        (z * plane + j, order[(r + 1) % len(order)] * plane + j)
        for r, z in enumerate(order)
        for j in range(plane)
    ]
    return lax.ppermute(value, "expert", pairs)


def turn(value, step):
    n = lax.axis_size("dp")
    return lax.ppermute(value, "dp", [((r + step) % n, r) for r in range(n)])


def after(value, *earlier):
    return lax.optimization_barrier((value, *earlier))[0]


def nt(a, b):
    return lax.dot_general(a, b, (((1,), (1,)), ((), ())), preferred_element_type=f32)


def tn(a, b):
    return lax.dot_general(a, b, (((0,), (0,)), ((), ())), preferred_element_type=f32)


class Pass:
    def __init__(self, tok, model, half, n_ex, n_dp, slots, blocks, last):
        self.tok, self.model, self.half, self.n_ex, self.n_dp = tok, model, half, n_ex, n_dp
        self.slots, self.blocks, self.last = slots, blocks, last
        self.layers = n_ex // plane
        self.rows = tok * len(blocks)
        self.width = model // n_dp

    def kernel(self, n_in, *refs):
        tok, model, half, rows, width = self.tok, self.model, self.half, self.rows, self.width
        n_dp, slots, blocks = self.n_dp, self.slots, self.blocks
        ins = dict(zip(self.names, refs[:n_in]))
        n_out = len(self.outs)
        outs = dict(zip(self.outs, refs[n_in : n_in + n_out]))
        scratch = list(refs[n_in + n_out :])
        xs, ys, ps, ws, gu, back, pre, sc, dx, pr, keep, send = scratch[:12]
        sem_t, sem_w, sem_i, sem_o = scratch[12:16]
        me_dp = lax.axis_index("dp")
        me = lax.axis_index("expert")
        here, layer = lax.rem(me, plane), lax.div(me, plane)

        def row_copies(b):
            ref, at = ins["t%d" % blocks[b]], pl.ds(b * tok, tok)
            cols = pl.ds(0, model)
            return (
                pltpu.make_async_copy(ref.at[pl.ds(0, tok), cols], xs.at[at], sem_t.at[b, 0]),
                pltpu.make_async_copy(ref.at[pl.ds(tok, tok), cols], ys.at[at], sem_t.at[b, 1]),
                pltpu.make_async_copy(
                    ref.at[pl.ds(0, tok), pl.ds(model, lanes)], ps.at[at], sem_t.at[b, 2]
                ),
            )

        for b in range(len(blocks)):
            for copy in row_copies(b):
                copy.start()

        def weight_copies(i):
            s = slots[i]
            if s == 0:
                return [pltpu.make_async_copy(ins["w0"], ws.at[i % 2], sem_w.at[i, 0])]
            out = []
            for k in range(n_dp):
                for h in range(2):
                    at = lax.rem(me_dp + k, n_dp) * width + h * (width // 2)
                    at = pl.multiple_of(at, width // 2)
                    out.append(
                        pltpu.make_async_copy(
                            ins["w%d_%d_%d" % (s, k, h)],
                            ws.at[i % 2, pl.ds(at, width // 2)],
                            sem_w.at[i, 2 * k + h],
                        )
                    )
            return out

        for copy in weight_copies(0):
            copy.start()
        extra = []
        held = {"dx": 0, "pr": 0, "keep": 0, "send": 0}
        for name, ref in ins.items():
            kind = name[0][:-1] if isinstance(name, tuple) and name[0][:-1] in held else None
            if kind is None:
                continue
            n = ref.shape[0]
            to = {"dx": dx, "pr": pr, "keep": keep, "send": send}[kind].at[pl.ds(held[kind], n)]
            extra.append(pltpu.make_async_copy(ref, to, sem_i.at[len(extra)]))
            held[kind] += n
        if not held["pr"]:
            pr[...] = jnp.zeros_like(pr)
        for copy in extra:
            copy.start()

        for b in range(len(blocks)):
            for copy in row_copies(b):
                copy.wait()
        chunk = min(128, tok)
        lane = lax.broadcasted_iota(jnp.int32, (chunk, lanes), 1)
        pending = []

        for i, s in enumerate(slots):
            for copy in weight_copies(i):
                copy.wait()
            if i + 1 < len(slots):
                for copy in weight_copies(i + 1):
                    copy.start()
            w = ws.at[i % 2]
            for n in range(0, 2 * half, tile):
                gu[:, n : n + tile] = jnp.dot(
                    xs[...], w[:, n : n + tile], preferred_element_type=f32
                )
            back[...] = jnp.dot(ys[...], w[:, 2 * half :], preferred_element_type=f32)
            if i == 0:
                for copy in extra:
                    copy.wait()
            expert = layer * plane + lax.bitwise_xor(here, jnp.int32(s))

            @pl.loop(0, rows // chunk)
            def _(r):
                at = pl.ds(pl.multiple_of(r * chunk, chunk), chunk)
                gate, upper, h = gu[at, :half], gu[at, half:], back[at, :]
                hit = lane == expert
                p = jnp.sum(jnp.where(hit, ps[at, :].astype(f32), 0.0), axis=1, keepdims=True)
                sigma = jax.nn.sigmoid(gate)
                silu = gate * sigma
                hidden = (silu * upper).astype(bf16).astype(f32)
                pair = jnp.sum(hidden * h, axis=1, keepdims=True)
                pr[at, :] += jnp.where(hit, pair, 0.0)
                grad = p * h
                pre[at, :half] = (grad * upper * (sigma * (1.0 + gate * (1.0 - sigma)))).astype(bf16)
                pre[at, half:] = (grad * silu).astype(bf16)
                sc[at, :] = (p * hidden).astype(bf16)

            add_dx = held["dx"] or i > 0
            for d in range(0, model, 2 * tile):
                at = slice(d, d + 2 * tile)
                part = nt(pre[...], w[at, : 2 * half])
                dx[:, at] = dx[:, at] + part if add_dx else part
            for d in range(0, width, 2 * tile):
                at = slice(d, d + 2 * tile)
                col = pl.ds(pl.multiple_of(me_dp * width + d, tile), 2 * tile)
                part = tn(sc[...], ys[:, col])
                keep[i, :, at] = keep[i, :, at] + part if held["keep"] else part
                for k in range(1, n_dp):
                    col = lax.rem(me_dp + n_dp - k, n_dp) * width + d
                    part = tn(sc[...], ys[:, pl.ds(pl.multiple_of(col, tile), 2 * tile)])
                    if held["send"]:
                        part = send[i, k - 1, :, at].astype(f32) + part
                    send[i, k - 1, :, at] = part.astype(bf16)

            pending.append(
                pltpu.make_async_copy(keep.at[i], outs["keep"].at[i], sem_o.at[2 * i])
            )
            pending.append(
                pltpu.make_async_copy(send.at[i], outs["send"].at[i], sem_o.at[2 * i + 1])
            )
            pending[-2].start()
            pending[-1].start()
        n = 2 * len(slots)
        if not self.last:
            pending.append(pltpu.make_async_copy(dx, outs["dx"], sem_o.at[n]))
            pending.append(pltpu.make_async_copy(pr, outs["pr"], sem_o.at[n + 1]))
            pending[-2].start()
            pending[-1].start()
        else:
            rows_out = scratch[16]
            for b, k in enumerate(blocks):
                at = pl.ds(b * tok, tok)
                rows_out[b, :, pl.ds(0, model)] = dx[at, :].astype(bf16)
                rows_out[b, :, pl.ds(model, lanes)] = pr[at, :].astype(bf16)
                copy = pltpu.make_async_copy(rows_out.at[b], outs["back"].at[k], sem_o.at[n + b])
                copy.start()
                pending.append(copy)
        for copy in pending:
            copy.wait()

    def call(self, ins):
        tok, model, half, rows, width = self.tok, self.model, self.half, self.rows, self.width
        n_dp, n = self.n_dp, len(self.slots)
        shape = {"keep": ((n, half, width), f32)}
        shape["send"] = ((n, max(n_dp - 1, 1), half, width), bf16)
        if self.last:
            shape["back"] = ((self.layers, tok, model + lanes), bf16)
        else:
            shape["dx"] = ((rows, model), f32)
            shape["pr"] = ((rows, lanes), f32)
        self.names, self.outs = list(ins), list(shape)
        scratch = [
            pltpu.VMEM((rows, model), bf16),
            pltpu.VMEM((rows, model), bf16),
            pltpu.VMEM((rows, lanes), bf16),
            pltpu.VMEM((min(n, 2), model, 3 * half), bf16),
            pltpu.VMEM((rows, 2 * half), f32),
            pltpu.VMEM((rows, half), f32),
            pltpu.VMEM((rows, 2 * half), bf16),
            pltpu.VMEM((rows, half), bf16),
            pltpu.VMEM((rows, model), f32),
            pltpu.VMEM((rows, lanes), f32),
            pltpu.VMEM((n, half, width), f32),
            pltpu.VMEM((n, max(n_dp - 1, 1), half, width), bf16),
            pltpu.SemaphoreType.DMA((len(self.blocks), 3)),
            pltpu.SemaphoreType.DMA((n, 2 * n_dp)),
            pltpu.SemaphoreType.DMA((8,)),
            pltpu.SemaphoreType.DMA((2 * n + len(self.blocks) + 2,)),
        ]
        if self.last:
            scratch.append(pltpu.VMEM((self.layers, tok, model + lanes), bf16))
        out = pl.pallas_call(
            functools.partial(self.kernel, len(ins)),
            out_shape=[jax.ShapeDtypeStruct(*v) for v in shape.values()],
            in_specs=[pl.BlockSpec(memory_space=pl.ANY)] * len(ins),
            out_specs=[pl.BlockSpec(memory_space=pl.ANY)] * len(shape),
            scratch_shapes=scratch,
            compiler_params=pltpu.CompilerParams(vmem_limit_bytes=56 * 2**20),
            cost_estimate=pl.CostEstimate(flops=1000, bytes_accessed=1000, transcendentals=0),
        )(*ins.values())
        return dict(zip(shape, out))


def adam_kernel(n_dp, lead_ref, *refs):
    grads = refs[:n_dp]
    m_ref, v_ref, w_ref, m_out, v_out, w_out = refs[n_dp:]
    me_dp = lax.axis_index("dp")
    width = grads[0].shape[1]
    is_lead = lead_ref[0] == me_dp
    for k, ref in enumerate(grads):
        at = lax.rem(me_dp + k, n_dp) * width
        at = pl.ds(pl.multiple_of(at, width), width)
        m_old, v_old = m_ref[0, 0, :, at], v_ref[0, 0, :, at]
        m_new, v_new, w_new = adam_update(ref[...].astype(f32), m_old, v_old, w_ref[0, :, at])
        m_out[0, 0, :, at] = jnp.where(is_lead, m_new, m_old)
        v_out[0, 0, :, at] = jnp.where(is_lead, v_new, v_old)
        w_out[:, at] = w_new


def adam_call(parts, leader, moment_one, moment_two, w_down):
    half, model = w_down.shape[1:]
    step = 48 if half % 48 == 0 else half
    n_dp = len(parts)
    width = model // n_dp
    wide = pl.BlockSpec((1, 1, step, model), lambda i: (0, 0, i, 0))
    return pl.pallas_call(
        functools.partial(adam_kernel, n_dp),
        grid=(half // step,),
        out_shape=[
            jax.ShapeDtypeStruct(moment_one.shape, f32),
            jax.ShapeDtypeStruct(moment_two.shape, f32),
            jax.ShapeDtypeStruct((half, model), bf16),
        ],
        in_specs=[pl.BlockSpec(memory_space=pltpu.SMEM)]
        + [pl.BlockSpec((step, width), lambda i: (i, 0))] * n_dp
        + [wide, wide, pl.BlockSpec((1, step, model), lambda i: (0, i, 0))],
        out_specs=[wide, wide, pl.BlockSpec((step, model), lambda i: (i, 0))],
        compiler_params=pltpu.CompilerParams(vmem_limit_bytes=32 * 2**20),
        cost_estimate=pl.CostEstimate(
            flops=1000, bytes_accessed=1000, transcendentals=0
        ),
    )(leader, *parts, moment_one, moment_two, w_down)


def body(
    tokens, out_grad, routes, probs, w_gate_up, w_down, moment_one, moment_two, replicas, leader
):
    tok_dev, model = tokens.shape
    half = w_down.shape[1]
    n_dp = lax.axis_size("dp")
    n_ex = lax.axis_size("expert")
    layers = n_ex // plane
    width = model // n_dp
    me_dp = lax.axis_index("dp")
    def others(value):
        return [turn(value, k) for k in range(1, n_dp)]

    wide = probs.astype(f32)
    ids = jnp.arange(lanes, dtype=jnp.int32)
    chosen = routes[:, :, None] == ids[None, None, :]
    p_all = jnp.sum(jnp.where(chosen, wide[:, :, None], 0.0), axis=1).astype(bf16)
    own = jnp.concatenate(
        [
            jnp.concatenate([tokens, p_all], 1),
            jnp.concatenate([out_grad, jnp.zeros_like(p_all)], 1),
        ],
        0,
    )
    w_gu, w_dn = w_gate_up[0], w_down[0]
    w_own = jnp.concatenate([w_gu, w_dn.T], 1)
    p1 = lax.dynamic_slice_in_dim(w_own, me_dp * width, width // 2, 0)
    p2 = lax.dynamic_slice_in_dim(w_own, me_dp * width + width // 2, width // 2, 0)
    held = [own, along(own)]
    x_p1, y_p2 = hop(p1, 1), hop(p2, 2)

    p1, p2, held, x_p1, y_p2 = lax.optimization_barrier((p1, p2, held, x_p1, y_p2))
    x_p2, y_p1 = hop(p2, 1), hop(p1, 2)
    while len(held) < layers - 1:
        held.append(along(held[-1]))
    x_o1, y_o2 = others(x_p1), others(y_p2)

    (x_p1, y_p2, x_p2, y_p1, x_o1, y_o2, held) = lax.optimization_barrier(
        (x_p1, y_p2, x_p2, y_p1, x_o1, y_o2, held)
    )
    d_p2, d_p1 = hop(y_p2, 1), hop(x_p1, 2)
    final = along(held[-1])
    x_o2, y_o1 = others(x_p2), others(y_p1)
    weights = {"w0": w_own}

    def name_parts(s, firsts, seconds):
        for k in range(n_dp):
            weights["w%d_%d_0" % (s, k)] = firsts[k]
            weights["w%d_%d_1" % (s, k)] = seconds[k]

    name_parts(1, [x_p1] + x_o1, [x_p2] + x_o2)
    name_parts(2, [y_p1] + y_o1, [y_p2] + y_o2)

    def pick(slots, blocks):
        got = {"t%d" % k: held[k] for k in blocks}
        for name, value in weights.items():
            if int(name[1]) in slots:
                got[name] = value
        return got

    near, far = list(range(layers - 1)), [layers - 1]
    make = functools.partial(Pass, tok_dev, model, half, n_ex, n_dp)

    def carry(*passes):
        return {(k + str(i), i): p[k] for i, (p, keys) in enumerate(passes) for k in keys}

    zero = make([0], near, False).call(pick([0], near))
    one = make([1, 2], near, False).call(pick([1, 2], near) | carry((zero, ("dx", "pr"))))

    zero, one, d_p1, d_p2, held, final = lax.optimization_barrier(
        (zero, one, d_p1, d_p2, held, final)
    )
    held.append(final)
    d_o1 = others(d_p1)
    d_o2 = others(d_p2)
    name_parts(3, [d_p1] + d_o1, [d_p2] + d_o2)
    grads = ("keep", "send")
    two = make([0, 1, 2], far, False).call(pick([0, 1, 2], far) | carry((zero, grads), (one, grads)))
    last = make([3], near + far, True).call(
        pick([3], near + far) | carry((one, ("dx", "pr")), (two, ("dx", "pr")))
    )

    swapped = [turn(two["send"][:, k - 1], k) for k in range(1, n_dp)]
    last, swapped, keep = lax.optimization_barrier((last, swapped, two["keep"]))
    leaving = [(keep[s] + sum(v[s].astype(f32) for v in swapped)).astype(bf16) for s in (1, 2)]
    leaving, last = lax.optimization_barrier((leaving, last))
    sent = [hop(leaving[0], 1), hop(leaving[1], 2)]
    swapped_across = [turn(last["send"][0, k - 1], k) for k in range(1, n_dp)]
    across = last["keep"][0] + sum(v.astype(f32) for v in swapped_across)
    across = across.astype(bf16)
    sent.append(hop(across, 3))
    back = last["back"]
    passing = along(back[1])
    for k in range(2, layers):
        passing = (passing.astype(f32) + back[k].astype(f32)).astype(bf16)
        passing = along(after(passing, across) if k == 2 else passing)

    sent, passing = lax.optimization_barrier((sent, passing))
    grad = keep[0] + sum(v[0].astype(f32) for v in swapped)
    grad = (grad + sum(v.astype(f32) for v in sent)).astype(bf16)
    parts = [grad] + others(grad)
    new_one, new_two, w_new = adam_call(parts, leader, moment_one, moment_two, w_down)
    lead = leader[0]
    fresh = w_new
    for k in range(1, n_dp):
        fresh = jnp.where((me_dp + k) % n_dp == lead, turn(w_new, k), fresh)

    total = back[0].astype(f32) + passing.astype(f32)
    token_grad = total[:, :model].astype(bf16)
    pair = total[:, model:]
    prob_grad = jnp.sum(jnp.where(chosen, pair[:, None, :], 0.0), axis=2).astype(bf16)
    is_live = replicas[0][me_dp] == 1
    new_down = jnp.where(is_live, fresh, w_dn)[None, None]
    return (token_grad, prob_grad, new_down, new_one, new_two)


def solution(mesh):
    in_specs = (
        P(("dp", "expert"), None),
        P(("dp", "expert"), None),
        P(("dp", "expert"), None),
        P(("dp", "expert"), None),
        P("expert", None, None),
        P("expert", None, None),
        P("dp", "expert", None, None),
        P("dp", "expert", None, None),
        P("expert", None),
        P("expert"),
    )
    out_specs = (
        P(("dp", "expert"), None),
        P(("dp", "expert"), None),
        P("dp", "expert", None, None),
        P("dp", "expert", None, None),
        P("dp", "expert", None, None),
    )
    return jax.shard_map(body, mesh=mesh, in_specs=in_specs, out_specs=out_specs, check_vma=False)
```

```python
import functools
import jax
import jax.numpy as jnp
from jax import lax
from jax.experimental import pallas as pl
from jax.experimental.pallas import tpu as pltpu
from jax.sharding import PartitionSpec as P

learn_rate = 0.01
beta_one = 0.9
beta_two = 0.95
adam_eps = 1e-08
weight_decay = 0.1
adam_step = 100

f32 = jnp.float32
bf16 = jnp.bfloat16
plane = 4
lanes = 128
tile = 256


def adam_update(grad, m_old, v_old, w_old):
    m_new = beta_one * m_old + (1.0 - beta_one) * grad
    v_new = beta_two * v_old + (1.0 - beta_two) * grad * grad
    m_hat = m_new / (1.0 - beta_one**adam_step)
    v_hat = v_new / (1.0 - beta_two**adam_step)
    w_wide = w_old.astype(f32)
    w_new = (
        w_wide - learn_rate * (m_hat / (jnp.sqrt(v_hat) + adam_eps) + weight_decay * w_wide)
    ).astype(bf16)
    return (m_new, v_new, w_new)


def hop(value, flip):
    n = lax.axis_size("expert")
    return lax.ppermute(value, "expert", [(i, i ^ flip) for i in range(n)])


def ring(layers):
    return [z for z in range(layers) if z == 0 or z % 2] + [
        z for z in range(layers - 1, 0, -1) if z % 2 == 0
    ]


def along(value):
    n = lax.axis_size("expert")
    order = ring(n // plane)
    pairs = [
        (z * plane + j, order[(r + 1) % len(order)] * plane + j)
        for r, z in enumerate(order)
        for j in range(plane)
    ]
    return lax.ppermute(value, "expert", pairs)


def turn(value, step):
    n = lax.axis_size("dp")
    return lax.ppermute(value, "dp", [((r + step) % n, r) for r in range(n)])


def after(value, *earlier):
    return lax.optimization_barrier((value, *earlier))[0]


def nt(a, b):
    return lax.dot_general(a, b, (((1,), (1,)), ((), ())), preferred_element_type=f32)


def tn(a, b):
    return lax.dot_general(a, b, (((0,), (0,)), ((), ())), preferred_element_type=f32)


class Pass:
    def __init__(self, tok, model, half, n_dp, slots, blocks, spans, back=False):
        self.tok, self.model, self.half, self.n_dp = tok, model, half, n_dp
        self.slots, self.blocks, self.spans, self.back = slots, blocks, spans, back
        self.rows = tok * len(blocks)
        self.width = model // n_dp

    def kernel(self, n_in, *refs):
        tok, model, half, rows, width = self.tok, self.model, self.half, self.rows, self.width
        n_dp, slots, blocks = self.n_dp, self.slots, self.blocks
        ins = dict(zip(self.names, refs[:n_in]))
        n_out = len(self.outs)
        outs = dict(zip(self.outs, refs[n_in : n_in + n_out]))
        scratch = list(refs[n_in + n_out :])
        xs, ys, ps, ws, gu, hs, pre, sc, dx, pr, keep, send = scratch[:12]
        sem_t, sem_w, sem_i, sem_k, sem_o = scratch[12:17]
        me_dp = lax.axis_index("dp")
        me = lax.axis_index("expert")
        here, layer = lax.rem(me, plane), lax.div(me, plane)

        def row_copies(b):
            ref, at = ins["t%d" % blocks[b]], pl.ds(b * tok, tok)
            cols = pl.ds(0, model)
            return (
                pltpu.make_async_copy(ref.at[pl.ds(0, tok), cols], xs.at[at], sem_t.at[b, 0]),
                pltpu.make_async_copy(ref.at[pl.ds(tok, tok), cols], ys.at[at], sem_t.at[b, 1]),
                pltpu.make_async_copy(
                    ref.at[pl.ds(0, tok), pl.ds(model, lanes)], ps.at[at], sem_t.at[b, 2]
                ),
            )

        def weight_copies(i):
            s = slots[i]
            if s == 0:
                return [pltpu.make_async_copy(ins["w0"], ws.at[i % 2], sem_w.at[i, 0])]
            out = []
            for k in range(n_dp):
                for h in range(2):
                    at = lax.rem(me_dp + k, n_dp) * width + h * (width // 2)
                    at = pl.multiple_of(at, width // 2)
                    out.append(
                        pltpu.make_async_copy(
                            ins["w%d_%d_%d" % (s, k, h)],
                            ws.at[i % 2, pl.ds(at, width // 2)],
                            sem_w.at[i, 2 * k + h],
                        )
                    )
            return out

        for b in range(len(blocks)):
            for copy in row_copies(b):
                copy.start()
        for copy in weight_copies(0):
            copy.start()
        extra = []
        for b, place in enumerate(self.sums):
            at = pl.ds(b * tok, tok)
            if place is None:
                dx[at, :] = jnp.zeros((tok, model), f32)
                pr[at, :] = jnp.zeros((tok, lanes), f32)
                continue
            j, row = place
            came = pl.ds(row * tok, tok)
            extra.append(
                pltpu.make_async_copy(ins["dx%d" % j].at[came], dx.at[at], sem_i.at[b, 0])
            )
            extra.append(
                pltpu.make_async_copy(ins["pr%d" % j].at[came], pr.at[at], sem_i.at[b, 1])
            )
        filled = 0
        for j in range(self.n_grads):
            n = ins["keep%d" % j].shape[0]
            at = pl.ds(filled, n)
            extra.append(pltpu.make_async_copy(ins["keep%d" % j], keep.at[at], sem_k.at[j, 0]))
            extra.append(pltpu.make_async_copy(ins["send%d" % j], send.at[at], sem_k.at[j, 1]))
            filled += n
        for copy in extra:
            copy.start()

        for b in range(len(blocks)):
            for copy in row_copies(b):
                copy.wait()
        chunk = min(128, tok)
        lane = lax.broadcasted_iota(jnp.int32, (chunk, lanes), 1)
        pending = []

        for i, s in enumerate(slots):
            for copy in weight_copies(i):
                copy.wait()
            if i + 1 < len(slots):
                for copy in weight_copies(i + 1):
                    copy.start()
            w = ws.at[i % 2]
            low, high = (tok * b for b in self.spans[i])
            mine = slice(low, high)
            for n in range(0, 2 * half, tile):
                gu[mine, n : n + tile] = jnp.dot(
                    xs[mine, :], w[:, n : n + tile], preferred_element_type=f32
                )
            hs[mine, :] = jnp.dot(ys[mine, :], w[:, 2 * half :], preferred_element_type=f32)
            if i == 0:
                for copy in extra:
                    copy.wait()
            expert = layer * plane + lax.bitwise_xor(here, jnp.int32(s))

            @pl.loop(low // chunk, high // chunk)
            def _(r):
                at = pl.ds(pl.multiple_of(r * chunk, chunk), chunk)
                gate, upper, h = gu[at, :half], gu[at, half:], hs[at, :]
                hit = lane == expert
                p = jnp.sum(jnp.where(hit, ps[at, :].astype(f32), 0.0), axis=1, keepdims=True)
                sigma = jax.nn.sigmoid(gate)
                silu = gate * sigma
                hidden = (silu * upper).astype(bf16).astype(f32)
                pair = jnp.sum(hidden * h, axis=1, keepdims=True)
                pr[at, :] += jnp.where(hit, pair, 0.0)
                grad = p * h
                pre[at, :half] = (grad * upper * (sigma * (1.0 + gate * (1.0 - sigma)))).astype(bf16)
                pre[at, half:] = (grad * silu).astype(bf16)
                sc[at, :] = (p * hidden).astype(bf16)

            for d in range(0, model, 2 * tile):
                at = slice(d, d + 2 * tile)
                dx[mine, at] = dx[mine, at] + nt(pre[mine, :], w[at, : 2 * half])
            for d in range(0, width, 2 * tile):
                at = slice(d, d + 2 * tile)
                col = pl.ds(pl.multiple_of(me_dp * width + d, tile), 2 * tile)
                part = tn(sc[mine, :], ys[mine, col])
                keep[i, :, at] = keep[i, :, at] + part if filled else part
                for k in range(1, n_dp):
                    col = lax.rem(me_dp + n_dp - k, n_dp) * width + d
                    col = pl.ds(pl.multiple_of(col, tile), 2 * tile)
                    part = tn(sc[mine, :], ys[mine, col])
                    if filled:
                        part = send[i, k - 1, :, at].astype(f32) + part
                    send[i, k - 1, :, at] = part.astype(bf16)

            pending.append(
                pltpu.make_async_copy(keep.at[i], outs["keep"].at[i], sem_o.at[2 * i])
            )
            pending.append(
                pltpu.make_async_copy(send.at[i], outs["send"].at[i], sem_o.at[2 * i + 1])
            )
            pending[-2].start()
            pending[-1].start()
        n = 2 * len(slots)
        if not self.back:
            pending.append(pltpu.make_async_copy(dx, outs["dx"], sem_o.at[n]))
            pending.append(pltpu.make_async_copy(pr, outs["pr"], sem_o.at[n + 1]))
            pending[-2].start()
            pending[-1].start()
        else:
            rows_out = scratch[17]
            for b in range(len(blocks)):
                at = pl.ds(b * tok, tok)
                rows_out[b, :, pl.ds(0, model)] = dx[at, :].astype(bf16)
                rows_out[b, :, pl.ds(model, lanes)] = pr[at, :].astype(bf16)
                copy = pltpu.make_async_copy(rows_out.at[b], outs["back"].at[b], sem_o.at[n + b])
                copy.start()
                pending.append(copy)
        for copy in pending:
            copy.wait()

    def call(self, ins, sums=(), grads=()):
        tok, model, half, rows, width = self.tok, self.model, self.half, self.rows, self.width
        n_dp, n = self.n_dp, len(self.slots)
        ins = dict(ins)
        self.sums = [None] * len(self.blocks)
        for j, (earlier, out) in enumerate(sums):
            for b, block in enumerate(self.blocks):
                if block in earlier.blocks:
                    self.sums[b] = (j, earlier.blocks.index(block))
            ins["dx%d" % j], ins["pr%d" % j] = out["dx"], out["pr"]
        self.n_grads = len(grads)
        for j, out in enumerate(grads):
            ins["keep%d" % j], ins["send%d" % j] = out["keep"], out["send"]
        shape = {"keep": ((n, half, width), f32)}
        shape["send"] = ((n, max(n_dp - 1, 1), half, width), bf16)
        out_rows = (len(self.blocks), tok, model + lanes)
        if self.back:
            shape["back"] = (out_rows, bf16)
        else:
            shape["dx"] = ((rows, model), f32)
            shape["pr"] = ((rows, lanes), f32)
        self.names, self.outs = list(ins), list(shape)
        scratch = [
            pltpu.VMEM((rows, model), bf16),
            pltpu.VMEM((rows, model), bf16),
            pltpu.VMEM((rows, lanes), bf16),
            pltpu.VMEM((min(n, 2), model, 3 * half), bf16),
            pltpu.VMEM((rows, 2 * half), f32),
            pltpu.VMEM((rows, half), f32),
            pltpu.VMEM((rows, 2 * half), bf16),
            pltpu.VMEM((rows, half), bf16),
            pltpu.VMEM((rows, model), f32),
            pltpu.VMEM((rows, lanes), f32),
            pltpu.VMEM((n, half, width), f32),
            pltpu.VMEM((n, max(n_dp - 1, 1), half, width), bf16),
            pltpu.SemaphoreType.DMA((len(self.blocks), 3)),
            pltpu.SemaphoreType.DMA((n, 2 * n_dp)),
            pltpu.SemaphoreType.DMA((len(self.blocks), 2)),
            pltpu.SemaphoreType.DMA((max(self.n_grads, 1), 2)),
            pltpu.SemaphoreType.DMA((2 * n + len(self.blocks) + 2,)),
        ]
        if self.back:
            scratch.append(pltpu.VMEM(out_rows, bf16))
        out = pl.pallas_call(
            functools.partial(self.kernel, len(ins)),
            out_shape=[jax.ShapeDtypeStruct(*v) for v in shape.values()],
            in_specs=[pl.BlockSpec(memory_space=pl.ANY)] * len(ins),
            out_specs=[pl.BlockSpec(memory_space=pl.ANY)] * len(shape),
            scratch_shapes=scratch,
            compiler_params=pltpu.CompilerParams(vmem_limit_bytes=56 * 2**20),
            cost_estimate=pl.CostEstimate(flops=1000, bytes_accessed=1000, transcendentals=0),
        )(*ins.values())
        return dict(zip(shape, out))


def adam_kernel(n_dp, lead_ref, *refs):
    grads = refs[:n_dp]
    m_ref, v_ref, w_ref, m_out, v_out, w_out = refs[n_dp:]
    me_dp = lax.axis_index("dp")
    width = grads[0].shape[1]
    is_lead = lead_ref[0] == me_dp
    for k, ref in enumerate(grads):
        at = lax.rem(me_dp + k, n_dp) * width
        at = pl.ds(pl.multiple_of(at, width), width)
        m_old, v_old = m_ref[0, 0, :, at], v_ref[0, 0, :, at]
        m_new, v_new, w_new = adam_update(ref[...].astype(f32), m_old, v_old, w_ref[0, :, at])
        m_out[0, 0, :, at] = jnp.where(is_lead, m_new, m_old)
        v_out[0, 0, :, at] = jnp.where(is_lead, v_new, v_old)
        w_out[:, at] = w_new


def adam_call(parts, leader, moment_one, moment_two, w_down):
    half, model = w_down.shape[1:]
    step = 48 if half % 48 == 0 else half
    n_dp = len(parts)
    width = model // n_dp
    wide = pl.BlockSpec((1, 1, step, model), lambda i: (0, 0, i, 0))
    return pl.pallas_call(
        functools.partial(adam_kernel, n_dp),
        grid=(half // step,),
        out_shape=[
            jax.ShapeDtypeStruct(moment_one.shape, f32),
            jax.ShapeDtypeStruct(moment_two.shape, f32),
            jax.ShapeDtypeStruct((half, model), bf16),
        ],
        in_specs=[pl.BlockSpec(memory_space=pltpu.SMEM)]
        + [pl.BlockSpec((step, width), lambda i: (i, 0))] * n_dp
        + [wide, wide, pl.BlockSpec((1, step, model), lambda i: (0, i, 0))],
        out_specs=[wide, wide, pl.BlockSpec((step, model), lambda i: (i, 0))],
        compiler_params=pltpu.CompilerParams(vmem_limit_bytes=32 * 2**20),
        cost_estimate=pl.CostEstimate(
            flops=1000, bytes_accessed=1000, transcendentals=0
        ),
    )(leader, *parts, moment_one, moment_two, w_down)


def body(
    tokens, out_grad, routes, probs, w_gate_up, w_down, moment_one, moment_two, replicas, leader
):
    tok_dev, model = tokens.shape
    half = w_down.shape[1]
    n_dp = lax.axis_size("dp")
    n_ex = lax.axis_size("expert")
    layers = n_ex // plane
    width = model // n_dp
    me_dp = lax.axis_index("dp")
    def others(value):
        return [turn(value, k) for k in range(1, n_dp)]

    wide = probs.astype(f32)
    ids = jnp.arange(lanes, dtype=jnp.int32)
    chosen = routes[:, :, None] == ids[None, None, :]
    p_all = jnp.sum(jnp.where(chosen, wide[:, :, None], 0.0), axis=1).astype(bf16)
    own = jnp.concatenate(
        [
            jnp.concatenate([tokens, p_all], 1),
            jnp.concatenate([out_grad, jnp.zeros_like(p_all)], 1),
        ],
        0,
    )
    w_gu, w_dn = w_gate_up[0], w_down[0]
    w_own = jnp.concatenate([w_gu, w_dn.T], 1)
    p1 = lax.dynamic_slice_in_dim(w_own, me_dp * width, width // 2, 0)
    p2 = lax.dynamic_slice_in_dim(w_own, me_dp * width + width // 2, width // 2, 0)
    held = [own, along(own)]
    x_p1, y_p2 = hop(p1, 1), hop(p2, 2)

    weights = {"w0": w_own}
    make = functools.partial(Pass, tok_dev, model, half, n_dp)
    last_block = layers - 1
    near = list(range(last_block))

    def pick(p):
        got = {"t%d" % k: held[k] for k in p.blocks}
        return got | {k: v for k, v in weights.items() if int(k[1]) in p.slots}

    def name_parts(s, firsts, seconds):
        for k in range(n_dp):
            weights["w%d_%d_0" % (s, k)] = firsts[k]
            weights["w%d_%d_1" % (s, k)] = seconds[k]

    p1, p2, held, x_p1, y_p2, w_own = lax.optimization_barrier((p1, p2, held, x_p1, y_p2, w_own))
    weights["w0"] = w_own
    x_p2, y_p1 = hop(p2, 1), hop(p1, 2)
    zero_pass = make([0], near[:2], [(0, 2)])
    zero = zero_pass.call(pick(zero_pass))
    while len(held) < layers - 1:
        held.append(along(held[-1]))
    x_o1, y_o2 = others(x_p1), others(y_p2)

    (x_p1, y_p2, x_p2, y_p1, x_o1, y_o2, held, zero) = lax.optimization_barrier(
        (x_p1, y_p2, x_p2, y_p1, x_o1, y_o2, held, zero)
    )
    d_p2, d_p1 = hop(y_p2, 1), hop(x_p1, 2)
    final = along(held[-1])
    x_o2, y_o1 = others(x_p2), others(y_p1)
    name_parts(1, [x_p1] + x_o1, [x_p2] + x_o2)
    name_parts(2, [y_p1] + y_o1, [y_p2] + y_o2)
    one_pass = make([1, 2], near, [(0, last_block)] * 2)
    one = one_pass.call(pick(one_pass), sums=[(zero_pass, zero)])

    zero, one, d_p1, d_p2, held, final = lax.optimization_barrier(
        (zero, one, d_p1, d_p2, held, final)
    )
    held.append(final)
    d_o1, d_o2 = others(d_p1), others(d_p2)
    name_parts(3, [d_p1] + d_o1, [d_p2] + d_o2)
    rest = list(range(2, layers))
    two_pass = make([0, 1, 2], rest, [(0, len(rest))] + [(len(rest) - 1, len(rest))] * 2)
    two = two_pass.call(pick(two_pass), sums=[(one_pass, one)], grads=[zero, one])
    two_send = after(two["send"], d_o1, d_o2)
    swapped = [turn(two_send[:, k - 1], k) for k in range(1, n_dp)]
    keep = two["keep"]
    sums = [(one_pass, one), (two_pass, two)]
    first_pass = make([3], [1], [(0, 1)], True)
    first = first_pass.call(pick(first_pass), sums=sums)
    first, swapped, keep = lax.optimization_barrier((first, swapped, keep))
    passing = along(first["back"][0])
    leaving = [(keep[s] + sum(v[s].astype(f32) for v in swapped)).astype(bf16) for s in (1, 2)]
    sent = [hop(leaving[0], 1), hop(leaving[1], 2)]
    others_pass = make([3], [0] + rest, [(0, len(rest) + 1)], True)
    last = others_pass.call(pick(others_pass), sums=sums, grads=[first])
    last, passing, sent = lax.optimization_barrier((last, passing, sent))

    back = last["back"]
    swapped_across = [turn(last["send"][0, k - 1], k) for k in range(1, n_dp)]
    across = last["keep"][0] + sum(v.astype(f32) for v in swapped_across)
    across = across.astype(bf16)
    sent.append(hop(across, 3))
    for k in range(2, layers):
        passing = (passing.astype(f32) + back[k - 1].astype(f32)).astype(bf16)
        passing = along(after(passing, across) if k == 3 else passing)

    sent, passing = lax.optimization_barrier((sent, passing))
    grad = keep[0] + sum(v[0].astype(f32) for v in swapped)
    grad = (grad + sum(v.astype(f32) for v in sent)).astype(bf16)
    parts = [grad] + others(grad)
    new_one, new_two, w_new = adam_call(parts, leader, moment_one, moment_two, w_down)
    lead = leader[0]
    fresh = w_new
    for k in range(1, n_dp):
        fresh = jnp.where((me_dp + k) % n_dp == lead, turn(w_new, k), fresh)

    total = back[0].astype(f32) + passing.astype(f32)
    token_grad = total[:, :model].astype(bf16)
    pair = total[:, model:]
    prob_grad = jnp.sum(jnp.where(chosen, pair[:, None, :], 0.0), axis=2).astype(bf16)
    is_live = replicas[0][me_dp] == 1
    new_down = jnp.where(is_live, fresh, w_dn)[None, None]
    return (token_grad, prob_grad, new_down, new_one, new_two)


def solution(mesh):
    in_specs = (
        P(("dp", "expert"), None),
        P(("dp", "expert"), None),
        P(("dp", "expert"), None),
        P(("dp", "expert"), None),
        P("expert", None, None),
        P("expert", None, None),
        P("dp", "expert", None, None),
        P("dp", "expert", None, None),
        P("expert", None),
        P("expert"),
    )
    out_specs = (
        P(("dp", "expert"), None),
        P(("dp", "expert"), None),
        P("dp", "expert", None, None),
        P("dp", "expert", None, None),
        P("dp", "expert", None, None),
    )
    return jax.shard_map(body, mesh=mesh, in_specs=in_specs, out_specs=out_specs, check_vma=False)
```

```python
import functools
import jax
import jax.numpy as jnp
from jax import lax
from jax.experimental import pallas as pl
from jax.experimental.pallas import tpu as pltpu
from jax.sharding import PartitionSpec as P

learn_rate = 0.01
beta_one = 0.9
beta_two = 0.95
adam_eps = 1e-08
weight_decay = 0.1
adam_step = 100

f32 = jnp.float32
bf16 = jnp.bfloat16
plane = 4
lanes = 128
tile = 256


def adam_update(grad, m_old, v_old, w_old):
    m_new = beta_one * m_old + (1.0 - beta_one) * grad
    v_new = beta_two * v_old + (1.0 - beta_two) * grad * grad
    m_hat = m_new / (1.0 - beta_one**adam_step)
    v_hat = v_new / (1.0 - beta_two**adam_step)
    w_wide = w_old.astype(f32)
    w_new = (
        w_wide - learn_rate * (m_hat / (jnp.sqrt(v_hat) + adam_eps) + weight_decay * w_wide)
    ).astype(bf16)
    return (m_new, v_new, w_new)


def hop(value, flip):
    n = lax.axis_size("expert")
    return lax.ppermute(value, "expert", [(i, i ^ flip) for i in range(n)])


def ring(layers):
    return [z for z in range(layers) if z == 0 or z % 2] + [
        z for z in range(layers - 1, 0, -1) if z % 2 == 0
    ]


def along(value):
    n = lax.axis_size("expert")
    order = ring(n // plane)
    pairs = [
        (z * plane + j, order[(r + 1) % len(order)] * plane + j)
        for r, z in enumerate(order)
        for j in range(plane)
    ]
    return lax.ppermute(value, "expert", pairs)


def turn(value, step):
    n = lax.axis_size("dp")
    return lax.ppermute(value, "dp", [((r + step) % n, r) for r in range(n)])


def after(value, *earlier):
    return lax.optimization_barrier((value, *earlier))[0]


def nt(a, b):
    return lax.dot_general(a, b, (((1,), (1,)), ((), ())), preferred_element_type=f32)


def tn(a, b):
    return lax.dot_general(a, b, (((0,), (0,)), ((), ())), preferred_element_type=f32)


class Pass:
    def __init__(self, tok, model, half, n_dp, slots, blocks, spans, back=0):
        self.tok, self.model, self.half, self.n_dp = tok, model, half, n_dp
        self.slots, self.blocks, self.spans, self.back = slots, blocks, spans, back
        self.left = blocks[back:]
        self.rows = tok * len(blocks)
        self.width = model // n_dp

    def kernel(self, n_in, *refs):
        tok, model, half, rows, width = self.tok, self.model, self.half, self.rows, self.width
        n_dp, slots, blocks = self.n_dp, self.slots, self.blocks
        ins = dict(zip(self.names, refs[:n_in]))
        n_out = len(self.outs)
        outs = dict(zip(self.outs, refs[n_in : n_in + n_out]))
        scratch = list(refs[n_in + n_out :])
        xs, ys, ps, ws, gu, hs, pre, sc, dx, pr, keep, send = scratch[:12]
        sem_t, sem_w, sem_i, sem_k, sem_o = scratch[12:17]
        me_dp = lax.axis_index("dp")
        me = lax.axis_index("expert")
        here, layer = lax.rem(me, plane), lax.div(me, plane)

        def row_copies(b):
            ref, at = ins["t%d" % blocks[b]], pl.ds(b * tok, tok)
            cols = pl.ds(0, model)
            return (
                pltpu.make_async_copy(ref.at[pl.ds(0, tok), cols], xs.at[at], sem_t.at[b, 0]),
                pltpu.make_async_copy(ref.at[pl.ds(tok, tok), cols], ys.at[at], sem_t.at[b, 1]),
                pltpu.make_async_copy(
                    ref.at[pl.ds(0, tok), pl.ds(model, lanes)], ps.at[at], sem_t.at[b, 2]
                ),
            )

        def weight_copies(i):
            s = slots[i]
            if s == 0:
                return [pltpu.make_async_copy(ins["w0"], ws.at[i % 2], sem_w.at[i, 0])]
            out = []
            for k in range(n_dp):
                for h in range(2):
                    at = lax.rem(me_dp + k, n_dp) * width + h * (width // 2)
                    at = pl.multiple_of(at, width // 2)
                    out.append(
                        pltpu.make_async_copy(
                            ins["w%d_%d_%d" % (s, k, h)],
                            ws.at[i % 2, pl.ds(at, width // 2)],
                            sem_w.at[i, 2 * k + h],
                        )
                    )
            return out

        for b in range(len(blocks)):
            for copy in row_copies(b):
                copy.start()
        for copy in weight_copies(0):
            copy.start()
        extra = []
        for b, place in enumerate(self.sums):
            at = pl.ds(b * tok, tok)
            if place is None:
                dx[at, :] = jnp.zeros((tok, model), f32)
                pr[at, :] = jnp.zeros((tok, lanes), f32)
                continue
            j, row = place
            came = pl.ds(row * tok, tok)
            extra.append(
                pltpu.make_async_copy(ins["dx%d" % j].at[came], dx.at[at], sem_i.at[b, 0])
            )
            extra.append(
                pltpu.make_async_copy(ins["pr%d" % j].at[came], pr.at[at], sem_i.at[b, 1])
            )
        filled = 0
        for j, (low, n) in enumerate(self.grads):
            at, came = pl.ds(filled, n), pl.ds(low, n)
            for name, ref, sem in (("keep", keep, 0), ("send", send, 1)):
                ref_in = ins["%s%d" % (name, j)].at[came]
                extra.append(pltpu.make_async_copy(ref_in, ref.at[at], sem_k.at[j, sem]))
            filled += n
        for copy in extra:
            copy.start()

        for b in range(len(blocks)):
            for copy in row_copies(b):
                copy.wait()
        chunk = min(128, tok)
        lane = lax.broadcasted_iota(jnp.int32, (chunk, lanes), 1)
        pending = []

        for i, s in enumerate(slots):
            for copy in weight_copies(i):
                copy.wait()
            if i + 1 < len(slots):
                for copy in weight_copies(i + 1):
                    copy.start()
            w = ws.at[i % 2]
            low, high = (tok * b for b in self.spans[i])
            mine = slice(low, high)
            for n in range(0, 2 * half, tile):
                gu[mine, n : n + tile] = jnp.dot(
                    xs[mine, :], w[:, n : n + tile], preferred_element_type=f32
                )
            hs[mine, :] = jnp.dot(ys[mine, :], w[:, 2 * half :], preferred_element_type=f32)
            if i == 0:
                for copy in extra:
                    copy.wait()
            expert = layer * plane + lax.bitwise_xor(here, jnp.int32(s))

            @pl.loop(low // chunk, high // chunk)
            def _(r):
                at = pl.ds(pl.multiple_of(r * chunk, chunk), chunk)
                gate, upper, h = gu[at, :half], gu[at, half:], hs[at, :]
                hit = lane == expert
                p = jnp.sum(jnp.where(hit, ps[at, :].astype(f32), 0.0), axis=1, keepdims=True)
                sigma = jax.nn.sigmoid(gate)
                silu = gate * sigma
                hidden = (silu * upper).astype(bf16).astype(f32)
                pair = jnp.sum(hidden * h, axis=1, keepdims=True)
                pr[at, :] += jnp.where(hit, pair, 0.0)
                grad = p * h
                pre[at, :half] = (grad * upper * (sigma * (1.0 + gate * (1.0 - sigma)))).astype(bf16)
                pre[at, half:] = (grad * silu).astype(bf16)
                sc[at, :] = (p * hidden).astype(bf16)

            for d in range(0, model, 2 * tile):
                at = slice(d, d + 2 * tile)
                dx[mine, at] = dx[mine, at] + nt(pre[mine, :], w[at, : 2 * half])
            for d in range(0, width, 2 * tile):
                at = slice(d, d + 2 * tile)
                col = pl.ds(pl.multiple_of(me_dp * width + d, tile), 2 * tile)
                part = tn(sc[mine, :], ys[mine, col])
                keep[i, :, at] = keep[i, :, at] + part if i < filled else part
                for k in range(1, n_dp):
                    col = lax.rem(me_dp + n_dp - k, n_dp) * width + d
                    col = pl.ds(pl.multiple_of(col, tile), 2 * tile)
                    part = tn(sc[mine, :], ys[mine, col])
                    if i < filled:
                        part = send[i, k - 1, :, at].astype(f32) + part
                    send[i, k - 1, :, at] = part.astype(bf16)

            pending.append(
                pltpu.make_async_copy(keep.at[i], outs["keep"].at[i], sem_o.at[2 * i])
            )
            pending.append(
                pltpu.make_async_copy(send.at[i], outs["send"].at[i], sem_o.at[2 * i + 1])
            )
            pending[-2].start()
            pending[-1].start()
        n = 2 * len(slots)
        if self.left:
            at = pl.ds(self.back * tok, len(self.left) * tok)
            pending.append(pltpu.make_async_copy(dx.at[at], outs["dx"], sem_o.at[n]))
            pending.append(pltpu.make_async_copy(pr.at[at], outs["pr"], sem_o.at[n + 1]))
            pending[-2].start()
            pending[-1].start()
        for b in range(self.back):
            rows_out = scratch[17]
            at = pl.ds(b * tok, tok)
            rows_out[b, :, pl.ds(0, model)] = dx[at, :].astype(bf16)
            rows_out[b, :, pl.ds(model, lanes)] = pr[at, :].astype(bf16)
            copy = pltpu.make_async_copy(rows_out.at[b], outs["back"].at[b], sem_o.at[n + 2 + b])
            copy.start()
            pending.append(copy)
        for copy in pending:
            copy.wait()

    def call(self, ins, sums=(), grads=()):
        tok, model, half, rows, width = self.tok, self.model, self.half, self.rows, self.width
        n_dp, n = self.n_dp, len(self.slots)
        ins = dict(ins)
        self.sums = [None] * len(self.blocks)
        for j, (earlier, out) in enumerate(sums):
            for b, block in enumerate(self.blocks):
                if block in earlier.left:
                    self.sums[b] = (j, earlier.left.index(block))
            ins["dx%d" % j], ins["pr%d" % j] = out["dx"], out["pr"]
        self.grads = [rows_from for _, rows_from in grads]
        for j, (out, _) in enumerate(grads):
            ins["keep%d" % j], ins["send%d" % j] = out["keep"], out["send"]
        shape = {"keep": ((n, half, width), f32)}
        shape["send"] = ((n, max(n_dp - 1, 1), half, width), bf16)
        out_rows = (self.back, tok, model + lanes)
        if self.back:
            shape["back"] = (out_rows, bf16)
        if self.left:
            shape["dx"] = ((len(self.left) * tok, model), f32)
            shape["pr"] = ((len(self.left) * tok, lanes), f32)
        self.names, self.outs = list(ins), list(shape)
        scratch = [
            pltpu.VMEM((rows, model), bf16),
            pltpu.VMEM((rows, model), bf16),
            pltpu.VMEM((rows, lanes), bf16),
            pltpu.VMEM((min(n, 2), model, 3 * half), bf16),
            pltpu.VMEM((rows, 2 * half), f32),
            pltpu.VMEM((rows, half), f32),
            pltpu.VMEM((rows, 2 * half), bf16),
            pltpu.VMEM((rows, half), bf16),
            pltpu.VMEM((rows, model), f32),
            pltpu.VMEM((rows, lanes), f32),
            pltpu.VMEM((n, half, width), f32),
            pltpu.VMEM((n, max(n_dp - 1, 1), half, width), bf16),
            pltpu.SemaphoreType.DMA((len(self.blocks), 3)),
            pltpu.SemaphoreType.DMA((n, 2 * n_dp)),
            pltpu.SemaphoreType.DMA((len(self.blocks), 2)),
            pltpu.SemaphoreType.DMA((max(len(self.grads), 1), 2)),
            pltpu.SemaphoreType.DMA((2 * n + len(self.blocks) + 2,)),
        ]
        if self.back:
            scratch.append(pltpu.VMEM(out_rows, bf16))
        out = pl.pallas_call(
            functools.partial(self.kernel, len(ins)),
            out_shape=[jax.ShapeDtypeStruct(*v) for v in shape.values()],
            in_specs=[pl.BlockSpec(memory_space=pl.ANY)] * len(ins),
            out_specs=[pl.BlockSpec(memory_space=pl.ANY)] * len(shape),
            scratch_shapes=scratch,
            compiler_params=pltpu.CompilerParams(vmem_limit_bytes=56 * 2**20),
            cost_estimate=pl.CostEstimate(flops=1000, bytes_accessed=1000, transcendentals=0),
        )(*ins.values())
        return dict(zip(shape, out))


def adam_kernel(n_dp, lead_ref, *refs):
    grads = refs[: 2 * n_dp]
    m_ref, v_ref, w_ref, m_out, v_out, w_out = refs[2 * n_dp :]
    upper = pl.program_id(0) < pl.num_programs(0) // 2
    me_dp = lax.axis_index("dp")
    width = grads[0].shape[1]
    is_lead = lead_ref[0] == me_dp
    for k in range(n_dp):
        grad = jnp.where(upper, grads[2 * k][...].astype(f32), grads[2 * k + 1][...].astype(f32))
        at = lax.rem(me_dp + k, n_dp) * width
        at = pl.ds(pl.multiple_of(at, width), width)
        m_old, v_old = m_ref[0, 0, :, at], v_ref[0, 0, :, at]
        m_new, v_new, w_new = adam_update(grad, m_old, v_old, w_ref[0, :, at])
        m_out[0, 0, :, at] = jnp.where(is_lead, m_new, m_old)
        v_out[0, 0, :, at] = jnp.where(is_lead, v_new, v_old)
        w_out[:, at] = w_new


def adam_call(parts, leader, moment_one, moment_two, w_down):
    half, model = w_down.shape[1:]
    step = 48 if half % 96 == 0 else half // 2
    steps = half // step
    n_dp = len(parts)
    width = model // n_dp
    wide = pl.BlockSpec((1, 1, step, model), lambda i: (0, 0, i, 0))
    return pl.pallas_call(
        functools.partial(adam_kernel, n_dp),
        grid=(steps,),
        out_shape=[
            jax.ShapeDtypeStruct(moment_one.shape, f32),
            jax.ShapeDtypeStruct(moment_two.shape, f32),
            jax.ShapeDtypeStruct((half, model), bf16),
        ],
        in_specs=[pl.BlockSpec(memory_space=pltpu.SMEM)]
        + [
            pl.BlockSpec((step, width), lambda i: (jnp.minimum(i, steps // 2 - 1), 0)),
            pl.BlockSpec((step, width), lambda i: (jnp.maximum(i - steps // 2, 0), 0)),
        ]
        * n_dp
        + [wide, wide, pl.BlockSpec((1, step, model), lambda i: (0, i, 0))],
        out_specs=[wide, wide, pl.BlockSpec((step, model), lambda i: (i, 0))],
        compiler_params=pltpu.CompilerParams(vmem_limit_bytes=32 * 2**20),
        cost_estimate=pl.CostEstimate(
            flops=1000, bytes_accessed=1000, transcendentals=0
        ),
    )(leader, *[v for pair in parts for v in pair], moment_one, moment_two, w_down)


def body(
    tokens, out_grad, routes, probs, w_gate_up, w_down, moment_one, moment_two, replicas, leader
):
    tok_dev, model = tokens.shape
    half = w_down.shape[1]
    n_dp = lax.axis_size("dp")
    n_ex = lax.axis_size("expert")
    layers = n_ex // plane
    width = model // n_dp
    me_dp = lax.axis_index("dp")
    def others(value):
        return [turn(value, k) for k in range(1, n_dp)]

    wide = probs.astype(f32)
    ids = jnp.arange(lanes, dtype=jnp.int32)
    chosen = routes[:, :, None] == ids[None, None, :]
    p_all = jnp.sum(jnp.where(chosen, wide[:, :, None], 0.0), axis=1).astype(bf16)
    own = jnp.concatenate(
        [
            jnp.concatenate([tokens, p_all], 1),
            jnp.concatenate([out_grad, jnp.zeros_like(p_all)], 1),
        ],
        0,
    )
    w_gu, w_dn = w_gate_up[0], w_down[0]
    w_own = jnp.concatenate([w_gu, w_dn.T], 1)
    p1 = lax.dynamic_slice_in_dim(w_own, me_dp * width, width // 2, 0)
    p2 = lax.dynamic_slice_in_dim(w_own, me_dp * width + width // 2, width // 2, 0)
    held = [own, along(own)]
    x_p1, y_p2 = hop(p1, 1), hop(p2, 2)

    weights = {"w0": w_own}
    make = functools.partial(Pass, tok_dev, model, half, n_dp)
    last_block = layers - 1
    near = list(range(last_block))

    def pick(p):
        got = {"t%d" % k: held[k] for k in p.blocks}
        return got | {k: v for k, v in weights.items() if int(k[1]) in p.slots}

    def name_parts(s, firsts, seconds):
        for k in range(n_dp):
            weights["w%d_%d_0" % (s, k)] = firsts[k]
            weights["w%d_%d_1" % (s, k)] = seconds[k]

    p1, p2, held, x_p1, y_p2, w_own = lax.optimization_barrier((p1, p2, held, x_p1, y_p2, w_own))
    weights["w0"] = w_own
    x_p2, y_p1 = hop(p2, 1), hop(p1, 2)
    zero_pass = make([0], near[:2], [(0, 2)])
    zero = zero_pass.call(pick(zero_pass))
    while len(held) < layers - 1:
        held.append(along(held[-1]))
    x_o1, y_o2 = others(x_p1), others(y_p2)

    (x_p1, y_p2, x_p2, y_p1, x_o1, y_o2, held, zero) = lax.optimization_barrier(
        (x_p1, y_p2, x_p2, y_p1, x_o1, y_o2, held, zero)
    )
    d_p2, d_p1 = hop(y_p2, 1), hop(x_p1, 2)
    final = along(held[-1])
    x_o2, y_o1 = others(x_p2), others(y_p1)
    name_parts(1, [x_p1] + x_o1, [x_p2] + x_o2)
    name_parts(2, [y_p1] + y_o1, [y_p2] + y_o2)
    one_pass = make([0, 1, 2], near, [(2, last_block)] + [(0, last_block)] * 2)
    one = one_pass.call(pick(one_pass), sums=[(zero_pass, zero)], grads=[(zero, (0, 1))])

    one, d_p1, d_p2, held, final = lax.optimization_barrier((one, d_p1, d_p2, held, final))
    held.append(final)
    d_o1, d_o2 = others(d_p1), others(d_p2)
    name_parts(3, [d_p1] + d_o1, [d_p2] + d_o2)
    two_pass = make([0, 1, 2], [last_block], [(0, 1)] * 3)
    two = two_pass.call(pick(two_pass), grads=[(one, (0, 3))])
    two_send = after(two["send"], d_o1, d_o2)
    swapped = [turn(two_send[:, k - 1], k) for k in range(1, n_dp)]
    keep = two["keep"]

    sums = [(one_pass, one), (two_pass, two)]
    early = near[1:]
    first_pass = make([3], early, [(0, len(early))], len(early))
    first = first_pass.call(pick(first_pass), sums=sums)
    first, swapped, keep = lax.optimization_barrier((first, swapped, keep))
    passing = along(first["back"][0])
    leaving = [(keep[s] + sum(v[s].astype(f32) for v in swapped)).astype(bf16) for s in (1, 2)]
    sent = [hop(leaving[0], 1), hop(leaving[1], 2)]
    rest_pass = make([3], [0, last_block], [(0, 2)], 2)
    last = rest_pass.call(pick(rest_pass), sums=sums, grads=[(first, (0, 1))])
    sent, last_keep, last_send = lax.optimization_barrier((sent, last["keep"], last["send"]))

    across = last_keep[0]
    for k in range(1, n_dp):
        across = across + turn(last_send[0, k - 1], k).astype(f32)
    sent.append(hop(across.astype(bf16), 3))
    for k in range(2, layers):
        term = first["back"][k - 1] if k < last_block else last["back"][1]
        passing = along((passing.astype(f32) + term.astype(f32)).astype(bf16))

    grad = keep[0] + sum(v[0].astype(f32) for v in swapped)
    grad = (grad + sum(v.astype(f32) for v in sent)).astype(bf16)
    cut = half // 2
    halves = [others(grad[:cut]), others(grad[cut:])]
    halves, passing = lax.optimization_barrier((halves, passing))
    parts = [(grad[:cut], grad[cut:])] + list(zip(*halves))
    new_one, new_two, w_new = adam_call(parts, leader, moment_one, moment_two, w_down)
    lead = leader[0]
    fresh = w_new
    for k in range(1, n_dp):
        fresh = jnp.where((me_dp + k) % n_dp == lead, turn(w_new, k), fresh)

    total = last["back"][0].astype(f32) + passing.astype(f32)
    token_grad = total[:, :model].astype(bf16)
    pair = total[:, model:]
    prob_grad = jnp.sum(jnp.where(chosen, pair[:, None, :], 0.0), axis=2).astype(bf16)
    is_live = replicas[0][me_dp] == 1
    new_down = jnp.where(is_live, fresh, w_dn)[None, None]
    return (token_grad, prob_grad, new_down, new_one, new_two)


def solution(mesh):
    in_specs = (
        P(("dp", "expert"), None),
        P(("dp", "expert"), None),
        P(("dp", "expert"), None),
        P(("dp", "expert"), None),
        P("expert", None, None),
        P("expert", None, None),
        P("dp", "expert", None, None),
        P("dp", "expert", None, None),
        P("expert", None),
        P("expert"),
    )
    out_specs = (
        P(("dp", "expert"), None),
        P(("dp", "expert"), None),
        P("dp", "expert", None, None),
        P("dp", "expert", None, None),
        P("dp", "expert", None, None),
    )
    return jax.shard_map(body, mesh=mesh, in_specs=in_specs, out_specs=out_specs, check_vma=False)
```

```python
import functools
import jax
import jax.numpy as jnp
from jax import lax
from jax.experimental import pallas as pl
from jax.experimental.pallas import tpu as pltpu
from jax.sharding import PartitionSpec as P

learn_rate = 0.01
beta_one = 0.9
beta_two = 0.95
adam_eps = 1e-08
weight_decay = 0.1
adam_step = 100

f32 = jnp.float32
bf16 = jnp.bfloat16
plane = 4
lanes = 128
tile = 256


def adam_update(grad, m_old, v_old, w_old):
    m_new = beta_one * m_old + (1.0 - beta_one) * grad
    v_new = beta_two * v_old + (1.0 - beta_two) * grad * grad
    m_hat = m_new / (1.0 - beta_one**adam_step)
    v_hat = v_new / (1.0 - beta_two**adam_step)
    w_wide = w_old.astype(f32)
    w_new = (
        w_wide - learn_rate * (m_hat / (jnp.sqrt(v_hat) + adam_eps) + weight_decay * w_wide)
    ).astype(bf16)
    return (m_new, v_new, w_new)


def hop(value, flip):
    n = lax.axis_size("expert")
    return lax.ppermute(value, "expert", [(i, i ^ flip) for i in range(n)])


def ring(layers):
    return [z for z in range(layers) if z == 0 or z % 2] + [
        z for z in range(layers - 1, 0, -1) if z % 2 == 0
    ]


def along(value):
    n = lax.axis_size("expert")
    order = ring(n // plane)
    pairs = [
        (z * plane + j, order[(r + 1) % len(order)] * plane + j)
        for r, z in enumerate(order)
        for j in range(plane)
    ]
    return lax.ppermute(value, "expert", pairs)


def turn(value, step):
    n = lax.axis_size("dp")
    return lax.ppermute(value, "dp", [((r + step) % n, r) for r in range(n)])


def after(value, *earlier):
    return lax.optimization_barrier((value, *earlier))[0]


def nt(a, b):
    return lax.dot_general(a, b, (((1,), (1,)), ((), ())), preferred_element_type=f32)


def tn(a, b):
    return lax.dot_general(a, b, (((0,), (0,)), ((), ())), preferred_element_type=f32)


class Pass:
    def __init__(self, tok, model, half, n_dp, slots, blocks, spans, back=0):
        self.tok, self.model, self.half, self.n_dp = tok, model, half, n_dp
        self.slots, self.blocks, self.spans, self.back = slots, blocks, spans, back
        self.left = blocks[back:]
        self.rows = tok * len(blocks)
        self.width = model // n_dp

    def kernel(self, n_in, *refs):
        tok, model, half, rows, width = self.tok, self.model, self.half, self.rows, self.width
        n_dp, slots, blocks = self.n_dp, self.slots, self.blocks
        ins = dict(zip(self.names, refs[:n_in]))
        n_out = len(self.outs)
        outs = dict(zip(self.outs, refs[n_in : n_in + n_out]))
        scratch = list(refs[n_in + n_out :])
        xs, ys, ps, ws, gu, hs, pre, sc, dx, pr, keep, send = scratch[:12]
        sem_t, sem_w, sem_i, sem_k, sem_o = scratch[12:17]
        me_dp = lax.axis_index("dp")
        me = lax.axis_index("expert")
        here, layer = lax.rem(me, plane), lax.div(me, plane)

        def row_copies(b):
            ref, at = ins["t%d" % blocks[b]], pl.ds(b * tok, tok)
            cols = pl.ds(0, model)
            return (
                pltpu.make_async_copy(ref.at[pl.ds(0, tok), cols], xs.at[at], sem_t.at[b, 0]),
                pltpu.make_async_copy(ref.at[pl.ds(tok, tok), cols], ys.at[at], sem_t.at[b, 1]),
                pltpu.make_async_copy(
                    ref.at[pl.ds(0, tok), pl.ds(model, lanes)], ps.at[at], sem_t.at[b, 2]
                ),
            )

        def weight_copies(i):
            s = slots[i]
            if s == 0:
                return [pltpu.make_async_copy(ins["w0"], ws.at[i % 2], sem_w.at[i, 0])]
            out = []
            for k in range(n_dp):
                for h in range(2):
                    at = lax.rem(me_dp + k, n_dp) * width + h * (width // 2)
                    at = pl.multiple_of(at, width // 2)
                    out.append(
                        pltpu.make_async_copy(
                            ins["w%d_%d_%d" % (s, k, h)],
                            ws.at[i % 2, pl.ds(at, width // 2)],
                            sem_w.at[i, 2 * k + h],
                        )
                    )
            return out

        for b in range(len(blocks)):
            for copy in row_copies(b):
                copy.start()
        for copy in weight_copies(0):
            copy.start()
        extra = []
        for b, place in enumerate(self.sums):
            at = pl.ds(b * tok, tok)
            if place is None:
                dx[at, :] = jnp.zeros((tok, model), f32)
                pr[at, :] = jnp.zeros((tok, lanes), f32)
                continue
            j, row = place
            came = pl.ds(row * tok, tok)
            extra.append(
                pltpu.make_async_copy(ins["dx%d" % j].at[came], dx.at[at], sem_i.at[b, 0])
            )
            extra.append(
                pltpu.make_async_copy(ins["pr%d" % j].at[came], pr.at[at], sem_i.at[b, 1])
            )
        filled = 0
        for j, (low, n) in enumerate(self.grads):
            at, came = pl.ds(filled, n), pl.ds(low, n)
            for name, ref, sem in (("keep", keep, 0), ("send", send, 1)):
                ref_in = ins["%s%d" % (name, j)].at[came]
                extra.append(pltpu.make_async_copy(ref_in, ref.at[at], sem_k.at[j, sem]))
            filled += n
        for copy in extra:
            copy.start()

        for b in range(len(blocks)):
            for copy in row_copies(b):
                copy.wait()
        chunk = min(128, tok)
        lane = lax.broadcasted_iota(jnp.int32, (chunk, lanes), 1)
        pending = []

        for i, s in enumerate(slots):
            for copy in weight_copies(i):
                copy.wait()
            if i + 1 < len(slots):
                for copy in weight_copies(i + 1):
                    copy.start()
            w = ws.at[i % 2]
            low, high = (tok * b for b in self.spans[i])
            mine = slice(low, high)
            for n in range(0, 2 * half, tile):
                gu[mine, n : n + tile] = jnp.dot(
                    xs[mine, :], w[:, n : n + tile], preferred_element_type=f32
                )
            hs[mine, :] = jnp.dot(ys[mine, :], w[:, 2 * half :], preferred_element_type=f32)
            if i == 0:
                for copy in extra:
                    copy.wait()
            expert = layer * plane + lax.bitwise_xor(here, jnp.int32(s))

            @pl.loop(low // chunk, high // chunk)
            def _(r):
                at = pl.ds(pl.multiple_of(r * chunk, chunk), chunk)
                gate, upper, h = gu[at, :half], gu[at, half:], hs[at, :]
                hit = lane == expert
                p = jnp.sum(jnp.where(hit, ps[at, :].astype(f32), 0.0), axis=1, keepdims=True)
                sigma = jax.nn.sigmoid(gate)
                silu = gate * sigma
                hidden = (silu * upper).astype(bf16).astype(f32)
                pair = jnp.sum(hidden * h, axis=1, keepdims=True)
                pr[at, :] += jnp.where(hit, pair, 0.0)
                grad = p * h
                pre[at, :half] = (grad * upper * (sigma * (1.0 + gate * (1.0 - sigma)))).astype(bf16)
                pre[at, half:] = (grad * silu).astype(bf16)
                sc[at, :] = (p * hidden).astype(bf16)

            for d in range(0, model, 2 * tile):
                at = slice(d, d + 2 * tile)
                dx[mine, at] = dx[mine, at] + nt(pre[mine, :], w[at, : 2 * half])
            for d in range(0, width, 2 * tile):
                at = slice(d, d + 2 * tile)
                col = pl.ds(pl.multiple_of(me_dp * width + d, tile), 2 * tile)
                part = tn(sc[mine, :], ys[mine, col])
                keep[i, :, at] = keep[i, :, at] + part if i < filled else part
                for k in range(1, n_dp):
                    col = lax.rem(me_dp + n_dp - k, n_dp) * width + d
                    col = pl.ds(pl.multiple_of(col, tile), 2 * tile)
                    part = tn(sc[mine, :], ys[mine, col])
                    if i < filled:
                        part = send[i, k - 1, :, at].astype(f32) + part
                    send[i, k - 1, :, at] = part.astype(bf16)

            pending.append(
                pltpu.make_async_copy(keep.at[i], outs["keep"].at[i], sem_o.at[2 * i])
            )
            pending.append(
                pltpu.make_async_copy(send.at[i], outs["send"].at[i], sem_o.at[2 * i + 1])
            )
            pending[-2].start()
            pending[-1].start()
        n = 2 * len(slots)
        if self.left:
            at = pl.ds(self.back * tok, len(self.left) * tok)
            pending.append(pltpu.make_async_copy(dx.at[at], outs["dx"], sem_o.at[n]))
            pending.append(pltpu.make_async_copy(pr.at[at], outs["pr"], sem_o.at[n + 1]))
            pending[-2].start()
            pending[-1].start()
        for b in range(self.back):
            rows_out = scratch[17]
            at = pl.ds(b * tok, tok)
            rows_out[b, :, pl.ds(0, model)] = dx[at, :].astype(bf16)
            rows_out[b, :, pl.ds(model, lanes)] = pr[at, :].astype(bf16)
            copy = pltpu.make_async_copy(rows_out.at[b], outs["back%d" % b], sem_o.at[n + 2 + b])
            copy.start()
            pending.append(copy)
        for copy in pending:
            copy.wait()

    def call(self, ins, sums=(), grads=()):
        tok, model, half, rows, width = self.tok, self.model, self.half, self.rows, self.width
        n_dp, n = self.n_dp, len(self.slots)
        ins = dict(ins)
        self.sums = [None] * len(self.blocks)
        for j, (earlier, out) in enumerate(sums):
            for b, block in enumerate(self.blocks):
                if block in earlier.left:
                    self.sums[b] = (j, earlier.left.index(block))
            ins["dx%d" % j], ins["pr%d" % j] = out["dx"], out["pr"]
        self.grads = [rows_from for _, rows_from in grads]
        for j, (out, _) in enumerate(grads):
            ins["keep%d" % j], ins["send%d" % j] = out["keep"], out["send"]
        shape = {"keep": ((n, half, width), f32)}
        shape["send"] = ((n, max(n_dp - 1, 1), half, width), bf16)
        out_rows = (self.back, tok, model + lanes)
        if self.back:
            for b in range(self.back):
                shape["back%d" % b] = (out_rows[1:], bf16)
        if self.left:
            shape["dx"] = ((len(self.left) * tok, model), f32)
            shape["pr"] = ((len(self.left) * tok, lanes), f32)
        self.names, self.outs = list(ins), list(shape)
        scratch = [
            pltpu.VMEM((rows, model), bf16),
            pltpu.VMEM((rows, model), bf16),
            pltpu.VMEM((rows, lanes), bf16),
            pltpu.VMEM((min(n, 2), model, 3 * half), bf16),
            pltpu.VMEM((rows, 2 * half), f32),
            pltpu.VMEM((rows, half), f32),
            pltpu.VMEM((rows, 2 * half), bf16),
            pltpu.VMEM((rows, half), bf16),
            pltpu.VMEM((rows, model), f32),
            pltpu.VMEM((rows, lanes), f32),
            pltpu.VMEM((n, half, width), f32),
            pltpu.VMEM((n, max(n_dp - 1, 1), half, width), bf16),
            pltpu.SemaphoreType.DMA((len(self.blocks), 3)),
            pltpu.SemaphoreType.DMA((n, 2 * n_dp)),
            pltpu.SemaphoreType.DMA((len(self.blocks), 2)),
            pltpu.SemaphoreType.DMA((max(len(self.grads), 1), 2)),
            pltpu.SemaphoreType.DMA((2 * n + len(self.blocks) + 2,)),
        ]
        if self.back:
            scratch.append(pltpu.VMEM(out_rows, bf16))
        out = pl.pallas_call(
            functools.partial(self.kernel, len(ins)),
            out_shape=[jax.ShapeDtypeStruct(*v) for v in shape.values()],
            in_specs=[pl.BlockSpec(memory_space=pl.ANY)] * len(ins),
            out_specs=[pl.BlockSpec(memory_space=pl.ANY)] * len(shape),
            scratch_shapes=scratch,
            compiler_params=pltpu.CompilerParams(vmem_limit_bytes=56 * 2**20),
            cost_estimate=pl.CostEstimate(flops=1000, bytes_accessed=1000, transcendentals=0),
        )(*ins.values())
        return dict(zip(shape, out))


def adam_kernel(n_dp, lead_ref, *refs):
    grads = refs[: 2 * n_dp]
    m_ref, v_ref, w_ref, m_out, v_out, w_out = refs[2 * n_dp :]
    upper = pl.program_id(0) < pl.num_programs(0) // 2
    me_dp = lax.axis_index("dp")
    width = grads[0].shape[1]
    is_lead = lead_ref[0] == me_dp
    for k in range(n_dp):
        grad = jnp.where(upper, grads[2 * k][...].astype(f32), grads[2 * k + 1][...].astype(f32))
        at = lax.rem(me_dp + k, n_dp) * width
        at = pl.ds(pl.multiple_of(at, width), width)
        m_old, v_old = m_ref[0, 0, :, at], v_ref[0, 0, :, at]
        m_new, v_new, w_new = adam_update(grad, m_old, v_old, w_ref[0, :, at])
        m_out[0, 0, :, at] = jnp.where(is_lead, m_new, m_old)
        v_out[0, 0, :, at] = jnp.where(is_lead, v_new, v_old)
        w_out[:, at] = w_new


def adam_call(parts, leader, moment_one, moment_two, w_down):
    half, model = w_down.shape[1:]
    step = 48 if half % 96 == 0 else half // 2
    steps = half // step
    n_dp = len(parts)
    width = model // n_dp
    wide = pl.BlockSpec((1, 1, step, model), lambda i: (0, 0, i, 0))
    return pl.pallas_call(
        functools.partial(adam_kernel, n_dp),
        grid=(steps,),
        out_shape=[
            jax.ShapeDtypeStruct(moment_one.shape, f32),
            jax.ShapeDtypeStruct(moment_two.shape, f32),
            jax.ShapeDtypeStruct((half, model), bf16),
        ],
        in_specs=[pl.BlockSpec(memory_space=pltpu.SMEM)]
        + [
            pl.BlockSpec((step, width), lambda i: (jnp.minimum(i, steps // 2 - 1), 0)),
            pl.BlockSpec((step, width), lambda i: (jnp.maximum(i - steps // 2, 0), 0)),
        ]
        * n_dp
        + [wide, wide, pl.BlockSpec((1, step, model), lambda i: (0, i, 0))],
        out_specs=[wide, wide, pl.BlockSpec((step, model), lambda i: (i, 0))],
        compiler_params=pltpu.CompilerParams(vmem_limit_bytes=32 * 2**20),
        cost_estimate=pl.CostEstimate(
            flops=1000, bytes_accessed=1000, transcendentals=0
        ),
    )(leader, *[v for pair in parts for v in pair], moment_one, moment_two, w_down)


def body(
    tokens, out_grad, routes, probs, w_gate_up, w_down, moment_one, moment_two, replicas, leader
):
    tok_dev, model = tokens.shape
    half = w_down.shape[1]
    n_dp = lax.axis_size("dp")
    n_ex = lax.axis_size("expert")
    layers = n_ex // plane
    width = model // n_dp
    me_dp = lax.axis_index("dp")
    def others(value):
        return [turn(value, k) for k in range(1, n_dp)]

    w_gu, w_dn = w_gate_up[0], w_down[0]
    w_own = jnp.concatenate([w_gu, w_dn.T], 1)
    p1 = lax.dynamic_slice_in_dim(w_own, me_dp * width, width // 2, 0)
    p2 = lax.dynamic_slice_in_dim(w_own, me_dp * width + width // 2, width // 2, 0)
    wide = after(probs, p1, p2).astype(f32)
    ids = jnp.arange(lanes, dtype=jnp.int32)
    chosen = routes[:, :, None] == ids[None, None, :]
    p_all = jnp.sum(jnp.where(chosen, wide[:, :, None], 0.0), axis=1).astype(bf16)
    own = jnp.concatenate(
        [
            jnp.concatenate([tokens, p_all], 1),
            jnp.concatenate([out_grad, jnp.zeros_like(p_all)], 1),
        ],
        0,
    )
    held = [own, along(own)]
    x_p1, y_p2, x_p2, y_p1 = hop(p1, 1), hop(p2, 2), hop(p2, 1), hop(p1, 2)

    weights = {"w0": w_own}
    make = functools.partial(Pass, tok_dev, model, half, n_dp)
    last_block = layers - 1
    near = list(range(last_block))

    def pick(p):
        got = {"t%d" % k: held[k] for k in p.blocks}
        return got | {k: v for k, v in weights.items() if int(k[1]) in p.slots}

    def name_parts(s, firsts, seconds):
        for k in range(n_dp):
            weights["w%d_%d_0" % (s, k)] = firsts[k]
            weights["w%d_%d_1" % (s, k)] = seconds[k]

    held, w_own, x_p1, y_p2 = lax.optimization_barrier((held, w_own, x_p1, y_p2))
    x_o1, y_o2 = others(x_p1), others(y_p2)
    weights["w0"] = w_own
    zero_pass = make([0], near[:2], [(0, 2)])
    zero = zero_pass.call(pick(zero_pass))
    while len(held) < layers - 1:
        held.append(along(held[-1]))

    x_p1, y_p2, x_p2, y_p1, x_o1, y_o2, held, zero = lax.optimization_barrier(
        (x_p1, y_p2, x_p2, y_p1, x_o1, y_o2, held, zero)
    )
    d_p2, d_p1 = hop(y_p2, 1), hop(x_p1, 2)
    final = along(held[-1])
    x_o2, y_o1 = others(x_p2), others(y_p1)
    name_parts(1, [x_p1] + x_o1, [x_p2] + x_o2)
    name_parts(2, [y_p1] + y_o1, [y_p2] + y_o2)
    one_pass = make([0, 1, 2], near, [(2, last_block)] + [(0, last_block)] * 2)
    one = one_pass.call(pick(one_pass), sums=[(zero_pass, zero)], grads=[(zero, (0, 1))])

    one, d_p1, d_p2, held, final = lax.optimization_barrier((one, d_p1, d_p2, held, final))
    held.append(final)
    d_o1, d_o2 = others(d_p1), others(d_p2)
    name_parts(3, [d_p1] + d_o1, [d_p2] + d_o2)
    two_pass = make([0, 1, 2], [last_block], [(0, 1)] * 3)
    two = two_pass.call(pick(two_pass), grads=[(one, (0, 3))])
    two_send = after(two["send"], d_o1, d_o2)
    swapped = [turn(two_send[:, k - 1], k) for k in range(1, n_dp)]
    keep = two["keep"]

    sums = [(one_pass, one), (two_pass, two)]
    early = near[1:]
    first_pass = make([3], early, [(0, len(early))], len(early))
    first = first_pass.call(pick(first_pass), sums=sums)
    first, swapped, keep = lax.optimization_barrier((first, swapped, keep))
    passing = along(first["back0"])
    cut = half // 2
    rows_of = [slice(0, cut), slice(cut, half)]

    def leaving(r, keep, swapped):
        total = [keep[s][r] + sum(v[s][r].astype(f32) for v in swapped) for s in (1, 2)]
        return [hop(total[0].astype(bf16), 1), hop(total[1].astype(bf16), 2)]

    sent = leaving(rows_of[0], keep, swapped)
    rest_pass = make([3], [0, last_block], [(0, 2)], 2)
    last = rest_pass.call(pick(rest_pass), sums=sums, grads=[(first, (0, 1))])
    sent, last_keep, last_send, keep, swapped = lax.optimization_barrier(
        (sent, last["keep"], last["send"], keep, swapped)
    )

    across = last_keep[0]
    for k in range(1, n_dp):
        across = across + turn(last_send[0, k - 1], k).astype(f32)
    sent_late = leaving(rows_of[1], keep, swapped)
    sent_across = hop(across.astype(bf16), 3)
    for k in range(2, layers):
        term = first["back%d" % (k - 1)] if k < last_block else last["back1"]
        if k == last_block:
            sent_late[0], passing = lax.optimization_barrier((sent_late[0], passing))
        passing = along((passing.astype(f32) + term.astype(f32)).astype(bf16))

    grads = []
    for r, came in zip(rows_of, (sent, sent_late)):
        grad = keep[0][r] + sum(v[0][r].astype(f32) for v in swapped)
        grad = grad + sum(v.astype(f32) for v in came) + sent_across[r].astype(f32)
        grads.append(grad.astype(bf16))
    halves = [others(grad) for grad in grads]
    halves, passing = lax.optimization_barrier((halves, passing))
    parts = [tuple(grads)] + list(zip(*halves))
    new_one, new_two, w_new = adam_call(parts, leader, moment_one, moment_two, w_down)
    lead = leader[0]
    fresh = w_new
    for k in range(1, n_dp):
        fresh = jnp.where((me_dp + k) % n_dp == lead, turn(w_new, k), fresh)

    total = last["back0"].astype(f32) + passing.astype(f32)
    token_grad = total[:, :model].astype(bf16)
    pair = total[:, model:]
    prob_grad = jnp.sum(jnp.where(chosen, pair[:, None, :], 0.0), axis=2).astype(bf16)
    is_live = replicas[0][me_dp] == 1
    new_down = jnp.where(is_live, fresh, w_dn)[None, None]
    return (token_grad, prob_grad, new_down, new_one, new_two)


def solution(mesh):
    in_specs = (
        P(("dp", "expert"), None),
        P(("dp", "expert"), None),
        P(("dp", "expert"), None),
        P(("dp", "expert"), None),
        P("expert", None, None),
        P("expert", None, None),
        P("dp", "expert", None, None),
        P("dp", "expert", None, None),
        P("expert", None),
        P("expert"),
    )
    out_specs = (
        P(("dp", "expert"), None),
        P(("dp", "expert"), None),
        P("dp", "expert", None, None),
        P("dp", "expert", None, None),
        P("dp", "expert", None, None),
    )
    return jax.shard_map(body, mesh=mesh, in_specs=in_specs, out_specs=out_specs, check_vma=False)
```

```python
import functools
import math
import jax
import jax.numpy as jnp
from jax import lax
from jax.experimental import pallas as pl
from jax.experimental.pallas import tpu as pltpu
from jax.sharding import PartitionSpec as P

learn_rate = 0.01
beta_one = 0.9
beta_two = 0.95
adam_eps = 1e-08
weight_decay = 0.1
adam_step = 100

f32 = jnp.float32
bf16 = jnp.bfloat16
plane = 4
lanes = 128
tile = 256


def adam_update(grad, m_old, v_old, w_old):
    m_new = beta_one * m_old + (1.0 - beta_one) * grad
    v_new = beta_two * v_old + (1.0 - beta_two) * grad * grad
    m_hat = m_new / (1.0 - beta_one**adam_step)
    v_hat = v_new / (1.0 - beta_two**adam_step)
    w_wide = w_old.astype(f32)
    w_new = (
        w_wide - learn_rate * (m_hat / (jnp.sqrt(v_hat) + adam_eps) + weight_decay * w_wide)
    ).astype(bf16)
    return (m_new, v_new, w_new)


def hop(value, flip):
    n = lax.axis_size("expert")
    return lax.ppermute(value, "expert", [(i, i ^ flip) for i in range(n)])


def ring(layers):
    return [z for z in range(layers) if z == 0 or z % 2] + [
        z for z in range(layers - 1, 0, -1) if z % 2 == 0
    ]


def along(value):
    n = lax.axis_size("expert")
    order = ring(n // plane)
    pairs = [
        (z * plane + j, order[(r + 1) % len(order)] * plane + j)
        for r, z in enumerate(order)
        for j in range(plane)
    ]
    return lax.ppermute(value, "expert", pairs)


def turn(value, step):
    n = lax.axis_size("dp")
    return lax.ppermute(value, "dp", [((r + step) % n, r) for r in range(n)])


def after(value, *earlier):
    return lax.optimization_barrier((value, *earlier))[0]


def nt(a, b):
    return lax.dot_general(a, b, (((1,), (1,)), ((), ())), preferred_element_type=f32)


def tn(a, b):
    return lax.dot_general(a, b, (((0,), (0,)), ((), ())), preferred_element_type=f32)


class Pass:
    def __init__(self, tok, model, half, n_dp, slots, blocks, spans, back=0):
        self.tok, self.model, self.half, self.n_dp = tok, model, half, n_dp
        self.slots, self.blocks, self.spans, self.back = slots, blocks, spans, back
        self.left = blocks[back:]
        self.rows = tok * len(blocks)
        self.width = model // n_dp

    def kernel(self, n_in, *refs):
        tok, model, half, rows, width = self.tok, self.model, self.half, self.rows, self.width
        n_dp, slots, blocks = self.n_dp, self.slots, self.blocks
        ins = dict(zip(self.names, refs[:n_in]))
        n_out = len(self.outs)
        outs = dict(zip(self.outs, refs[n_in : n_in + n_out]))
        scratch = list(refs[n_in + n_out :])
        xs, ys, ps, ws, gu, hs, pre, sc, dx, pr, keep, send = scratch[:12]
        sem_t, sem_w, sem_i, sem_k, sem_o = scratch[12:17]
        me_dp = lax.axis_index("dp")
        me = lax.axis_index("expert")
        here, layer = lax.rem(me, plane), lax.div(me, plane)

        def row_copies(b):
            ref, at = ins["t%d" % blocks[b]], pl.ds(b * tok, tok)
            first, second = pl.ds(0, model), pl.ds(model, model)
            return (
                pltpu.make_async_copy(ref.at[:, first], xs.at[at], sem_t.at[b, 0]),
                pltpu.make_async_copy(ref.at[:, second], ys.at[at], sem_t.at[b, 1]),
                pltpu.make_async_copy(
                    ref.at[:, pl.ds(2 * model, lanes)], ps.at[at], sem_t.at[b, 2]
                ),
            )

        def weight_copies(i):
            s = slots[i]
            if s == 0:
                return [pltpu.make_async_copy(ins["w0"], ws.at[i % 2], sem_w.at[i, 0])]
            out = []
            for k in range(n_dp):
                for h in range(2):
                    at = lax.rem(me_dp + k, n_dp) * width + h * (width // 2)
                    at = pl.multiple_of(at, width // 2)
                    out.append(
                        pltpu.make_async_copy(
                            ins["w%d_%d_%d" % (s, k, h)],
                            ws.at[i % 2, pl.ds(at, width // 2)],
                            sem_w.at[i, 2 * k + h],
                        )
                    )
            return out

        for b in range(len(blocks)):
            for copy in row_copies(b):
                copy.start()
        for copy in weight_copies(0):
            copy.start()
        extra = []
        for b, place in enumerate(self.sums):
            at = pl.ds(b * tok, tok)
            if place is None:
                dx[at, :] = jnp.zeros((tok, model), f32)
                pr[at, :] = jnp.zeros((tok, lanes), f32)
                continue
            j, row = place
            came = pl.ds(row * tok, tok)
            extra.append(
                pltpu.make_async_copy(ins["dx%d" % j].at[came], dx.at[at], sem_i.at[b, 0])
            )
            extra.append(
                pltpu.make_async_copy(ins["pr%d" % j].at[came], pr.at[at], sem_i.at[b, 1])
            )
        filled = 0
        for j, (low, n) in enumerate(self.grads):
            at, came = pl.ds(filled, n), pl.ds(low, n)
            for name, ref, sem in (("keep", keep, 0), ("send", send, 1)):
                ref_in = ins["%s%d" % (name, j)].at[came]
                extra.append(pltpu.make_async_copy(ref_in, ref.at[at], sem_k.at[j, sem]))
            filled += n
        for copy in extra:
            copy.start()

        for b in range(len(blocks)):
            for copy in row_copies(b):
                copy.wait()
        chunk = min(128, tok)
        lane = lax.broadcasted_iota(jnp.int32, (chunk, lanes), 1)
        pending = []

        for i, s in enumerate(slots):
            for copy in weight_copies(i):
                copy.wait()
            if i + 1 < len(slots):
                for copy in weight_copies(i + 1):
                    copy.start()
            w = ws.at[i % 2]
            low, high = (tok * b for b in self.spans[i])
            mine = slice(low, high)
            for n in range(0, 2 * half, tile):
                gu[mine, n : n + tile] = jnp.dot(
                    xs[mine, :], w[:, n : n + tile], preferred_element_type=f32
                )
            hs[mine, :] = jnp.dot(ys[mine, :], w[:, 2 * half :], preferred_element_type=f32)
            if i == 0:
                for copy in extra:
                    copy.wait()
            expert = layer * plane + lax.bitwise_xor(here, jnp.int32(s))

            @pl.loop(low // chunk, high // chunk)
            def _(r):
                at = pl.ds(pl.multiple_of(r * chunk, chunk), chunk)
                gate, upper, h = gu[at, :half], gu[at, half:], hs[at, :]
                hit = lane == expert
                p = jnp.sum(jnp.where(hit, ps[at, :].astype(f32), 0.0), axis=1, keepdims=True)
                sigma = jax.nn.sigmoid(gate)
                silu = gate * sigma
                hidden = (silu * upper).astype(bf16).astype(f32)
                pair = jnp.sum(hidden * h, axis=1, keepdims=True)
                pr[at, :] += jnp.where(hit, pair, 0.0)
                grad = p * h
                pre[at, :half] = (grad * upper * (sigma * (1.0 + gate * (1.0 - sigma)))).astype(bf16)
                pre[at, half:] = (grad * silu).astype(bf16)
                sc[at, :] = (p * hidden).astype(bf16)

            for d in range(0, model, 2 * tile):
                at = slice(d, d + 2 * tile)
                dx[mine, at] = dx[mine, at] + nt(pre[mine, :], w[at, : 2 * half])
            for d in range(0, width, 2 * tile):
                at = slice(d, d + 2 * tile)
                col = pl.ds(pl.multiple_of(me_dp * width + d, tile), 2 * tile)
                part = tn(sc[mine, :], ys[mine, col])
                keep[i, :, at] = keep[i, :, at] + part if i < filled else part
                for k in range(1, n_dp):
                    col = lax.rem(me_dp + n_dp - k, n_dp) * width + d
                    col = pl.ds(pl.multiple_of(col, tile), 2 * tile)
                    part = tn(sc[mine, :], ys[mine, col])
                    if i < filled:
                        part = send[i, k - 1, :, at].astype(f32) + part
                    send[i, k - 1, :, at] = part.astype(bf16)

            pending.append(
                pltpu.make_async_copy(keep.at[i], outs["keep"].at[i], sem_o.at[2 * i])
            )
            pending.append(
                pltpu.make_async_copy(send.at[i], outs["send"].at[i], sem_o.at[2 * i + 1])
            )
            pending[-2].start()
            pending[-1].start()
        n = 2 * len(slots)
        if self.left:
            at = pl.ds(self.back * tok, len(self.left) * tok)
            pending.append(pltpu.make_async_copy(dx.at[at], outs["dx"], sem_o.at[n]))
            pending.append(pltpu.make_async_copy(pr.at[at], outs["pr"], sem_o.at[n + 1]))
            pending[-2].start()
            pending[-1].start()
        for b in range(self.back):
            rows_out = scratch[17]
            at = pl.ds(b * tok, tok)
            rows_out[b, :, pl.ds(0, model)] = dx[at, :].astype(bf16)
            rows_out[b, :, pl.ds(model, lanes)] = pr[at, :].astype(bf16)
            copy = pltpu.make_async_copy(rows_out.at[b], outs["back%d" % b], sem_o.at[n + 2 + b])
            copy.start()
            pending.append(copy)
        for copy in pending:
            copy.wait()

    def call(self, ins, sums=(), grads=()):
        tok, model, half, rows, width = self.tok, self.model, self.half, self.rows, self.width
        n_dp, n = self.n_dp, len(self.slots)
        ins = dict(ins)
        self.sums = [None] * len(self.blocks)
        for j, (earlier, out) in enumerate(sums):
            for b, block in enumerate(self.blocks):
                if block in earlier.left:
                    self.sums[b] = (j, earlier.left.index(block))
            ins["dx%d" % j], ins["pr%d" % j] = out["dx"], out["pr"]
        self.grads = [rows_from for _, rows_from in grads]
        for j, (out, _) in enumerate(grads):
            ins["keep%d" % j], ins["send%d" % j] = out["keep"], out["send"]
        shape = {"keep": ((n, half, width), f32)}
        shape["send"] = ((n, max(n_dp - 1, 1), half, width), bf16)
        out_rows = (self.back, tok, model + lanes)
        if self.back:
            for b in range(self.back):
                shape["back%d" % b] = (out_rows[1:], bf16)
        if self.left:
            shape["dx"] = ((len(self.left) * tok, model), f32)
            shape["pr"] = ((len(self.left) * tok, lanes), f32)
        self.names, self.outs = list(ins), list(shape)
        scratch = [
            pltpu.VMEM((rows, model), bf16),
            pltpu.VMEM((rows, model), bf16),
            pltpu.VMEM((rows, lanes), bf16),
            pltpu.VMEM((min(n, 2), model, 3 * half), bf16),
            pltpu.VMEM((rows, 2 * half), f32),
            pltpu.VMEM((rows, half), f32),
            pltpu.VMEM((rows, 2 * half), bf16),
            pltpu.VMEM((rows, half), bf16),
            pltpu.VMEM((rows, model), f32),
            pltpu.VMEM((rows, lanes), f32),
            pltpu.VMEM((n, half, width), f32),
            pltpu.VMEM((n, max(n_dp - 1, 1), half, width), bf16),
            pltpu.SemaphoreType.DMA((len(self.blocks), 3)),
            pltpu.SemaphoreType.DMA((n, 2 * n_dp)),
            pltpu.SemaphoreType.DMA((len(self.blocks), 2)),
            pltpu.SemaphoreType.DMA((max(len(self.grads), 1), 2)),
            pltpu.SemaphoreType.DMA((2 * n + len(self.blocks) + 2,)),
        ]
        if self.back:
            scratch.append(pltpu.VMEM(out_rows, bf16))
        out = pl.pallas_call(
            functools.partial(self.kernel, len(ins)),
            out_shape=[jax.ShapeDtypeStruct(*v) for v in shape.values()],
            in_specs=[pl.BlockSpec(memory_space=pl.ANY)] * len(ins),
            out_specs=[pl.BlockSpec(memory_space=pl.ANY)] * len(shape),
            scratch_shapes=scratch,
            compiler_params=pltpu.CompilerParams(vmem_limit_bytes=56 * 2**20),
            cost_estimate=pl.CostEstimate(flops=1000, bytes_accessed=1000, transcendentals=0),
        )(*ins.values())
        return dict(zip(shape, out))


def pack_kernel(n_dp, x_ref, y_ref, routes, probs, gu_ref, dn_ref, p1, p2, own, *scratch):
    wide, turned, rows, sem = scratch
    tok, model = x_ref.shape
    part, half = wide.shape[0], turned.shape[0]
    at = pl.ds(pl.multiple_of(lax.axis_index("dp") * part, part), part)
    copies = [
        pltpu.make_async_copy(dn_ref.at[0, :, at], turned, sem.at[0]),
        pltpu.make_async_copy(gu_ref.at[0, at], wide.at[:, pl.ds(0, 2 * half)], sem.at[1]),
        pltpu.make_async_copy(x_ref, rows.at[:, pl.ds(0, model)], sem.at[2]),
        pltpu.make_async_copy(y_ref, rows.at[:, pl.ds(model, model)], sem.at[3]),
    ]
    for copy in copies:
        copy.start()
    expert = lax.broadcasted_iota(jnp.int32, (lanes, tok), 0)
    named = jnp.zeros((lanes, tok), f32)
    p = probs[...].astype(f32)
    for k in range(routes.shape[0]):
        named = named + jnp.where(expert == routes[k : k + 1, :], p[k : k + 1, :], 0.0)
    rows[:, 2 * model :] = jnp.transpose(named).astype(bf16)
    copies[0].wait()
    wide[:, 2 * half :] = jnp.transpose(turned[...])
    copies[1].wait()
    first, second = pl.ds(0, part // 2), pl.ds(part // 2, part // 2)
    leaving = [
        pltpu.make_async_copy(wide.at[first], p1, sem.at[4]),
        pltpu.make_async_copy(wide.at[second], p2, sem.at[5]),
        pltpu.make_async_copy(rows, own, sem.at[6]),
    ]
    leaving[0].start()
    leaving[1].start()
    copies[2].wait()
    copies[3].wait()
    leaving[2].start()
    for copy in leaving:
        copy.wait()


def pack(tokens, out_grad, routes, probs, w_gate_up, w_down, n_dp):
    tok, model = tokens.shape
    half = w_down.shape[1]
    part = model // n_dp
    piece = jax.ShapeDtypeStruct((part // 2, 3 * half), bf16)
    anywhere, inside = pl.BlockSpec(memory_space=pl.ANY), pl.BlockSpec(memory_space=pltpu.VMEM)
    return pl.pallas_call(
        functools.partial(pack_kernel, n_dp),
        out_shape=[piece, piece, jax.ShapeDtypeStruct((tok, 2 * model + lanes), bf16)],
        in_specs=[anywhere, anywhere, inside, inside, anywhere, anywhere],
        out_specs=[anywhere] * 3,
        scratch_shapes=[
            pltpu.VMEM((part, 3 * half), bf16),
            pltpu.VMEM((half, part), bf16),
            pltpu.VMEM((tok, 2 * model + lanes), bf16),
            pltpu.SemaphoreType.DMA((7,)),
        ],
        compiler_params=pltpu.CompilerParams(vmem_limit_bytes=56 * 2**20),
        cost_estimate=pl.CostEstimate(flops=1000, bytes_accessed=1000, transcendentals=0),
    )(tokens, out_grad, routes.T, probs.T, w_gate_up, w_down)


def adam_kernel(n_dp, cut, lead_ref, *refs):
    grads = refs[: 2 * n_dp]
    m_ref, v_ref, w_ref, m_out, v_out, w_out = refs[2 * n_dp :]
    upper = pl.program_id(0) < cut
    me_dp = lax.axis_index("dp")
    width = grads[0].shape[1]
    is_lead = lead_ref[0] == me_dp
    for k in range(n_dp):
        grad = jnp.where(upper, grads[2 * k][...].astype(f32), grads[2 * k + 1][...].astype(f32))
        at = lax.rem(me_dp + k, n_dp) * width
        at = pl.ds(pl.multiple_of(at, width), width)
        m_old, v_old = m_ref[0, 0, :, at], v_ref[0, 0, :, at]
        m_new, v_new, w_new = adam_update(grad, m_old, v_old, w_ref[0, :, at])
        m_out[0, 0, :, at] = jnp.where(is_lead, m_new, m_old)
        v_out[0, 0, :, at] = jnp.where(is_lead, v_new, v_old)
        w_out[:, at] = w_new


def adam_call(parts, leader, moment_one, moment_two, w_down):
    half, model = w_down.shape[1:]
    step = math.gcd(64, math.gcd(*[part.shape[0] for part in parts[0]]))
    steps, cut = half // step, parts[0][0].shape[0] // step
    n_dp = len(parts)
    width = model // n_dp
    wide = pl.BlockSpec((1, 1, step, model), lambda i: (0, 0, i, 0))
    return pl.pallas_call(
        functools.partial(adam_kernel, n_dp, cut),
        grid=(steps,),
        out_shape=[
            jax.ShapeDtypeStruct(moment_one.shape, f32),
            jax.ShapeDtypeStruct(moment_two.shape, f32),
            jax.ShapeDtypeStruct((half, model), bf16),
        ],
        in_specs=[pl.BlockSpec(memory_space=pltpu.SMEM)]
        + [
            pl.BlockSpec((step, width), lambda i: (jnp.minimum(i, cut - 1), 0)),
            pl.BlockSpec((step, width), lambda i: (jnp.maximum(i - cut, 0), 0)),
        ]
        * n_dp
        + [wide, wide, pl.BlockSpec((1, step, model), lambda i: (0, i, 0))],
        out_specs=[wide, wide, pl.BlockSpec((step, model), lambda i: (i, 0))],
        compiler_params=pltpu.CompilerParams(vmem_limit_bytes=32 * 2**20),
        cost_estimate=pl.CostEstimate(
            flops=1000, bytes_accessed=1000, transcendentals=0
        ),
    )(leader, *[v for pair in parts for v in pair], moment_one, moment_two, w_down)


def body(
    tokens, out_grad, routes, probs, w_gate_up, w_down, moment_one, moment_two, replicas, leader
):
    tok_dev, model = tokens.shape
    half = w_down.shape[1]
    n_dp = lax.axis_size("dp")
    n_ex = lax.axis_size("expert")
    layers = n_ex // plane
    width = model // n_dp
    me_dp = lax.axis_index("dp")
    def others(value):
        return [turn(value, k) for k in range(1, n_dp)]

    p1, p2, own = pack(tokens, out_grad, routes, probs, w_gate_up, w_down, n_dp)
    w_gu, w_dn = w_gate_up[0], after(w_down, own)[0]
    w_own = jnp.concatenate([w_gu, w_dn.T], 1)
    held = [own, along(own)]
    x_p1, y_p2, x_p2, y_p1 = hop(p1, 1), hop(p2, 2), hop(p2, 1), hop(p1, 2)

    weights = {"w0": w_own}
    make = functools.partial(Pass, tok_dev, model, half, n_dp)
    last_block = layers - 1
    near = list(range(last_block))

    def pick(p):
        got = {"t%d" % k: held[k] for k in p.blocks}
        return got | {k: v for k, v in weights.items() if int(k[1]) in p.slots}

    def name_parts(s, firsts, seconds):
        for k in range(n_dp):
            weights["w%d_%d_0" % (s, k)] = firsts[k]
            weights["w%d_%d_1" % (s, k)] = seconds[k]

    held, w_own, x_p1, y_p2 = lax.optimization_barrier((held, w_own, x_p1, y_p2))
    x_o1, y_o2 = others(x_p1), others(y_p2)
    weights["w0"] = w_own
    zero_pass = make([0], near[:2], [(0, 2)])
    zero = zero_pass.call(pick(zero_pass))
    while len(held) < layers - 1:
        held.append(along(held[-1]))

    x_p1, y_p2, x_p2, y_p1, x_o1, y_o2, held, zero = lax.optimization_barrier(
        (x_p1, y_p2, x_p2, y_p1, x_o1, y_o2, held, zero)
    )
    d_p2, d_p1 = hop(y_p2, 1), hop(x_p1, 2)
    final = along(held[-1])
    x_o2, y_o1 = others(x_p2), others(y_p1)
    name_parts(1, [x_p1] + x_o1, [x_p2] + x_o2)
    name_parts(2, [y_p1] + y_o1, [y_p2] + y_o2)
    one_pass = make([0, 1, 2], near, [(2, last_block)] + [(0, last_block)] * 2)
    one = one_pass.call(pick(one_pass), sums=[(zero_pass, zero)], grads=[(zero, (0, 1))])

    one, d_p1, d_p2, held, final = lax.optimization_barrier((one, d_p1, d_p2, held, final))
    held.append(final)
    d_o1, d_o2 = others(d_p1), others(d_p2)
    name_parts(3, [d_p1] + d_o1, [d_p2] + d_o2)
    two_pass = make([0, 1, 2], [last_block], [(0, 1)] * 3)
    two = two_pass.call(pick(two_pass), grads=[(one, (0, 3))])
    two_send = after(two["send"], d_o1, d_o2)
    swapped = [turn(two_send[:, k - 1], k) for k in range(1, n_dp)]
    keep = two["keep"]

    sums = [(one_pass, one), (two_pass, two)]
    early = near[1:]
    first_pass = make([3], early, [(0, len(early))], len(early))
    first = first_pass.call(pick(first_pass), sums=sums)
    first, swapped, keep = lax.optimization_barrier((first, swapped, keep))
    passing = along(first["back0"])
    cut = half * 2 // 3
    rows_of = [slice(0, cut), slice(cut, half)]

    def leaving(r, keep, swapped):
        total = [keep[s][r] + sum(v[s][r].astype(f32) for v in swapped) for s in (1, 2)]
        return [hop(total[0].astype(bf16), 1), hop(total[1].astype(bf16), 2)]

    sent = leaving(rows_of[0], keep, swapped)
    rest_pass = make([3], [0, last_block], [(0, 2)], 2)
    last = rest_pass.call(pick(rest_pass), sums=sums, grads=[(first, (0, 1))])
    sent, last_keep, last_send, keep, swapped = lax.optimization_barrier(
        (sent, last["keep"], last["send"], keep, swapped)
    )

    across = last_keep[0]
    for k in range(1, n_dp):
        across = across + turn(last_send[0, k - 1], k).astype(f32)
    sent_late = leaving(rows_of[1], keep, swapped)
    sent_across = hop(across.astype(bf16), 3)
    for k in range(2, layers):
        term = first["back%d" % (k - 1)] if k < last_block else last["back1"]
        if k == last_block:
            sent_late[0], passing = lax.optimization_barrier((sent_late[0], passing))
        passing = along((passing.astype(f32) + term.astype(f32)).astype(bf16))

    grads = []
    for r, came in zip(rows_of, (sent, sent_late)):
        grad = keep[0][r] + sum(v[0][r].astype(f32) for v in swapped)
        grad = grad + sum(v.astype(f32) for v in came) + sent_across[r].astype(f32)
        grads.append(grad.astype(bf16))
    halves = [others(grad) for grad in grads]
    halves, passing = lax.optimization_barrier((halves, passing))
    parts = [tuple(grads)] + list(zip(*halves))
    new_one, new_two, w_new = adam_call(parts, leader, moment_one, moment_two, w_down)
    lead = leader[0]
    fresh = w_new
    for k in range(1, n_dp):
        fresh = jnp.where((me_dp + k) % n_dp == lead, turn(w_new, k), fresh)

    total = last["back0"].astype(f32) + passing.astype(f32)
    token_grad = total[:, :model].astype(bf16)
    pair = total[:, model:]
    chosen = routes[:, :, None] == jnp.arange(lanes, dtype=jnp.int32)[None, None, :]
    prob_grad = jnp.sum(jnp.where(chosen, pair[:, None, :], 0.0), axis=2).astype(bf16)
    is_live = replicas[0][me_dp] == 1
    new_down = jnp.where(is_live, fresh, w_dn)[None, None]
    return (token_grad, prob_grad, new_down, new_one, new_two)


def solution(mesh):
    in_specs = (
        P(("dp", "expert"), None),
        P(("dp", "expert"), None),
        P(("dp", "expert"), None),
        P(("dp", "expert"), None),
        P("expert", None, None),
        P("expert", None, None),
        P("dp", "expert", None, None),
        P("dp", "expert", None, None),
        P("expert", None),
        P("expert"),
    )
    out_specs = (
        P(("dp", "expert"), None),
        P(("dp", "expert"), None),
        P("dp", "expert", None, None),
        P("dp", "expert", None, None),
        P("dp", "expert", None, None),
    )
    return jax.shard_map(body, mesh=mesh, in_specs=in_specs, out_specs=out_specs, check_vma=False)
```

```python
import functools
import math
import jax
import jax.numpy as jnp
from jax import lax
from jax.experimental import pallas as pl
from jax.experimental.pallas import tpu as pltpu
from jax.sharding import PartitionSpec as P

learn_rate = 0.01
beta_one = 0.9
beta_two = 0.95
adam_eps = 1e-08
weight_decay = 0.1
adam_step = 100

f32 = jnp.float32
bf16 = jnp.bfloat16
plane = 4
lanes = 128
tile = 256


def adam_update(grad, m_old, v_old, w_old):
    m_new = beta_one * m_old + (1.0 - beta_one) * grad
    v_new = beta_two * v_old + (1.0 - beta_two) * grad * grad
    m_hat = m_new / (1.0 - beta_one**adam_step)
    v_hat = v_new / (1.0 - beta_two**adam_step)
    w_wide = w_old.astype(f32)
    w_new = (
        w_wide - learn_rate * (m_hat / (jnp.sqrt(v_hat) + adam_eps) + weight_decay * w_wide)
    ).astype(bf16)
    return (m_new, v_new, w_new)


def hop(value, flip):
    n = lax.axis_size("expert")
    return lax.ppermute(value, "expert", [(i, i ^ flip) for i in range(n)])


def ring(layers):
    return [z for z in range(layers) if z == 0 or z % 2] + [
        z for z in range(layers - 1, 0, -1) if z % 2 == 0
    ]


def along(value):
    n = lax.axis_size("expert")
    order = ring(n // plane)
    pairs = [
        (z * plane + j, order[(r + 1) % len(order)] * plane + j)
        for r, z in enumerate(order)
        for j in range(plane)
    ]
    return lax.ppermute(value, "expert", pairs)


def turn(value, step):
    n = lax.axis_size("dp")
    return lax.ppermute(value, "dp", [((r + step) % n, r) for r in range(n)])


def after(value, *earlier):
    return lax.optimization_barrier((value, *earlier))[0]


def nt(a, b):
    return lax.dot_general(a, b, (((1,), (1,)), ((), ())), preferred_element_type=f32)


def tn(a, b):
    return lax.dot_general(a, b, (((0,), (0,)), ((), ())), preferred_element_type=f32)


class Pass:
    def __init__(self, tok, model, half, n_dp, slots, blocks, spans, back=0):
        self.tok, self.model, self.half, self.n_dp = tok, model, half, n_dp
        self.slots, self.blocks, self.spans, self.back = slots, blocks, spans, back
        self.left = blocks[back:]
        self.rows = tok * len(blocks)
        self.width = model // n_dp

    def kernel(self, n_in, *refs):
        tok, model, half, rows, width = self.tok, self.model, self.half, self.rows, self.width
        n_dp, slots, blocks = self.n_dp, self.slots, self.blocks
        ins = dict(zip(self.names, refs[:n_in]))
        n_out = len(self.outs)
        outs = dict(zip(self.outs, refs[n_in : n_in + n_out]))
        scratch = list(refs[n_in + n_out :])
        xs, ys, ps, ws, gu, hs, pre, sc, dx, pr, keep, send = scratch[:12]
        sem_t, sem_w, sem_i, sem_k, sem_o = scratch[12:17]
        me_dp = lax.axis_index("dp")
        me = lax.axis_index("expert")
        here, layer = lax.rem(me, plane), lax.div(me, plane)

        def row_copies(b):
            ref, at = ins["t%d" % blocks[b]], pl.ds(b * tok, tok)
            first, second = pl.ds(0, model), pl.ds(model, model)
            return (
                pltpu.make_async_copy(ref.at[:, first], xs.at[at], sem_t.at[b, 0]),
                pltpu.make_async_copy(ref.at[:, second], ys.at[at], sem_t.at[b, 1]),
                pltpu.make_async_copy(
                    ref.at[:, pl.ds(2 * model, lanes)], ps.at[at], sem_t.at[b, 2]
                ),
            )

        def weight_copies(i):
            s = slots[i]
            if s == 0:
                return [pltpu.make_async_copy(ins["w0"], ws.at[i % 2], sem_w.at[i, 0])]
            out = []
            for k in range(n_dp):
                for h in range(2):
                    at = lax.rem(me_dp + k, n_dp) * width + h * (width // 2)
                    at = pl.multiple_of(at, width // 2)
                    out.append(
                        pltpu.make_async_copy(
                            ins["w%d_%d_%d" % (s, k, h)],
                            ws.at[i % 2, pl.ds(at, width // 2)],
                            sem_w.at[i, 2 * k + h],
                        )
                    )
            return out

        for b in range(len(blocks)):
            for copy in row_copies(b):
                copy.start()
        for copy in weight_copies(0):
            copy.start()
        extra = []
        for b, place in enumerate(self.sums):
            at = pl.ds(b * tok, tok)
            if place is None:
                dx[at, :] = jnp.zeros((tok, model), f32)
                pr[at, :] = jnp.zeros((tok, lanes), f32)
                continue
            j, row = place
            came = pl.ds(row * tok, tok)
            extra.append(
                pltpu.make_async_copy(ins["dx%d" % j].at[came], dx.at[at], sem_i.at[b, 0])
            )
            extra.append(
                pltpu.make_async_copy(ins["pr%d" % j].at[came], pr.at[at], sem_i.at[b, 1])
            )
        filled = 0
        for j, (low, n) in enumerate(self.grads):
            at, came = pl.ds(filled, n), pl.ds(low, n)
            for name, ref, sem in (("keep", keep, 0), ("send", send, 1)):
                ref_in = ins["%s%d" % (name, j)].at[came]
                extra.append(pltpu.make_async_copy(ref_in, ref.at[at], sem_k.at[j, sem]))
            filled += n
        for copy in extra:
            copy.start()

        for b in range(len(blocks)):
            for copy in row_copies(b):
                copy.wait()
        chunk = min(128, tok)
        lane = lax.broadcasted_iota(jnp.int32, (chunk, lanes), 1)
        pending = []

        for i, s in enumerate(slots):
            for copy in weight_copies(i):
                copy.wait()
            if i + 1 < len(slots):
                for copy in weight_copies(i + 1):
                    copy.start()
            w = ws.at[i % 2]
            low, high = (tok * b for b in self.spans[i])
            mine = slice(low, high)
            for n in range(0, 2 * half, tile):
                gu[mine, n : n + tile] = jnp.dot(
                    xs[mine, :], w[:, n : n + tile], preferred_element_type=f32
                )
            hs[mine, :] = jnp.dot(ys[mine, :], w[:, 2 * half :], preferred_element_type=f32)
            if i == 0:
                for copy in extra:
                    copy.wait()
            expert = layer * plane + lax.bitwise_xor(here, jnp.int32(s))

            @pl.loop(low // chunk, high // chunk)
            def _(r):
                at = pl.ds(pl.multiple_of(r * chunk, chunk), chunk)
                gate, upper, h = gu[at, :half], gu[at, half:], hs[at, :]
                hit = lane == expert
                p = jnp.sum(jnp.where(hit, ps[at, :].astype(f32), 0.0), axis=1, keepdims=True)
                sigma = jax.nn.sigmoid(gate)
                silu = gate * sigma
                hidden = (silu * upper).astype(bf16).astype(f32)
                pair = jnp.sum(hidden * h, axis=1, keepdims=True)
                pr[at, :] += jnp.where(hit, pair, 0.0)
                grad = p * h
                pre[at, :half] = (grad * upper * (sigma * (1.0 + gate * (1.0 - sigma)))).astype(bf16)
                pre[at, half:] = (grad * silu).astype(bf16)
                sc[at, :] = (p * hidden).astype(bf16)

            for d in range(0, model, 2 * tile):
                at = slice(d, d + 2 * tile)
                dx[mine, at] = dx[mine, at] + nt(pre[mine, :], w[at, : 2 * half])
            for d in range(0, width, 2 * tile):
                at = slice(d, d + 2 * tile)
                col = pl.ds(pl.multiple_of(me_dp * width + d, tile), 2 * tile)
                part = tn(sc[mine, :], ys[mine, col])
                keep[i, :, at] = keep[i, :, at] + part if i < filled else part
                for k in range(1, n_dp):
                    col = lax.rem(me_dp + n_dp - k, n_dp) * width + d
                    col = pl.ds(pl.multiple_of(col, tile), 2 * tile)
                    part = tn(sc[mine, :], ys[mine, col])
                    if i < filled:
                        part = send[i, k - 1, :, at].astype(f32) + part
                    send[i, k - 1, :, at] = part.astype(bf16)

            pending.append(
                pltpu.make_async_copy(keep.at[i], outs["keep"].at[i], sem_o.at[2 * i])
            )
            pending.append(
                pltpu.make_async_copy(send.at[i], outs["send"].at[i], sem_o.at[2 * i + 1])
            )
            pending[-2].start()
            pending[-1].start()
        n = 2 * len(slots)
        if self.left:
            at = pl.ds(self.back * tok, len(self.left) * tok)
            pending.append(pltpu.make_async_copy(dx.at[at], outs["dx"], sem_o.at[n]))
            pending.append(pltpu.make_async_copy(pr.at[at], outs["pr"], sem_o.at[n + 1]))
            pending[-2].start()
            pending[-1].start()
        for b in range(self.back):
            rows_out = scratch[17]
            at = pl.ds(b * tok, tok)
            rows_out[b, :, pl.ds(0, model)] = dx[at, :].astype(bf16)
            rows_out[b, :, pl.ds(model, lanes)] = pr[at, :].astype(bf16)
            copy = pltpu.make_async_copy(rows_out.at[b], outs["back%d" % b], sem_o.at[n + 2 + b])
            copy.start()
            pending.append(copy)
        for copy in pending:
            copy.wait()

    def call(self, ins, sums=(), grads=()):
        tok, model, half, rows, width = self.tok, self.model, self.half, self.rows, self.width
        n_dp, n = self.n_dp, len(self.slots)
        ins = dict(ins)
        self.sums = [None] * len(self.blocks)
        for j, (earlier, out) in enumerate(sums):
            for b, block in enumerate(self.blocks):
                if block in earlier.left:
                    self.sums[b] = (j, earlier.left.index(block))
            ins["dx%d" % j], ins["pr%d" % j] = out["dx"], out["pr"]
        self.grads = [rows_from for _, rows_from in grads]
        for j, (out, _) in enumerate(grads):
            ins["keep%d" % j], ins["send%d" % j] = out["keep"], out["send"]
        shape = {"keep": ((n, half, width), f32)}
        shape["send"] = ((n, max(n_dp - 1, 1), half, width), bf16)
        out_rows = (self.back, tok, model + lanes)
        if self.back:
            for b in range(self.back):
                shape["back%d" % b] = (out_rows[1:], bf16)
        if self.left:
            shape["dx"] = ((len(self.left) * tok, model), f32)
            shape["pr"] = ((len(self.left) * tok, lanes), f32)
        self.names, self.outs = list(ins), list(shape)
        scratch = [
            pltpu.VMEM((rows, model), bf16),
            pltpu.VMEM((rows, model), bf16),
            pltpu.VMEM((rows, lanes), bf16),
            pltpu.VMEM((min(n, 2), model, 3 * half), bf16),
            pltpu.VMEM((rows, 2 * half), f32),
            pltpu.VMEM((rows, half), f32),
            pltpu.VMEM((rows, 2 * half), bf16),
            pltpu.VMEM((rows, half), bf16),
            pltpu.VMEM((rows, model), f32),
            pltpu.VMEM((rows, lanes), f32),
            pltpu.VMEM((n, half, width), f32),
            pltpu.VMEM((n, max(n_dp - 1, 1), half, width), bf16),
            pltpu.SemaphoreType.DMA((len(self.blocks), 3)),
            pltpu.SemaphoreType.DMA((n, 2 * n_dp)),
            pltpu.SemaphoreType.DMA((len(self.blocks), 2)),
            pltpu.SemaphoreType.DMA((max(len(self.grads), 1), 2)),
            pltpu.SemaphoreType.DMA((2 * n + len(self.blocks) + 2,)),
        ]
        if self.back:
            scratch.append(pltpu.VMEM(out_rows, bf16))
        out = pl.pallas_call(
            functools.partial(self.kernel, len(ins)),
            out_shape=[jax.ShapeDtypeStruct(*v) for v in shape.values()],
            in_specs=[pl.BlockSpec(memory_space=pl.ANY)] * len(ins),
            out_specs=[pl.BlockSpec(memory_space=pl.ANY)] * len(shape),
            scratch_shapes=scratch,
            compiler_params=pltpu.CompilerParams(vmem_limit_bytes=56 * 2**20),
            cost_estimate=pl.CostEstimate(flops=1000, bytes_accessed=1000, transcendentals=0),
        )(*ins.values())
        return dict(zip(shape, out))


def pack_kernel(n_dp, x_ref, y_ref, routes, probs, gu_ref, dn_ref, p1, p2, own, *scratch):
    wide, turned, rows, sem = scratch
    tok, model = x_ref.shape
    part, half = wide.shape[0], turned.shape[0]
    at = pl.ds(pl.multiple_of(lax.axis_index("dp") * part, part), part)
    copies = [
        pltpu.make_async_copy(dn_ref.at[0, :, at], turned, sem.at[0]),
        pltpu.make_async_copy(gu_ref.at[0, at], wide.at[:, pl.ds(0, 2 * half)], sem.at[1]),
        pltpu.make_async_copy(x_ref, rows.at[:, pl.ds(0, model)], sem.at[2]),
        pltpu.make_async_copy(y_ref, rows.at[:, pl.ds(model, model)], sem.at[3]),
    ]
    for copy in copies:
        copy.start()
    expert = lax.broadcasted_iota(jnp.int32, (lanes, tok), 0)
    named = jnp.zeros((lanes, tok), f32)
    p = probs[...].astype(f32)
    for k in range(routes.shape[0]):
        named = named + jnp.where(expert == routes[k : k + 1, :], p[k : k + 1, :], 0.0)
    rows[:, 2 * model :] = jnp.transpose(named).astype(bf16)
    copies[0].wait()
    wide[:, 2 * half :] = jnp.transpose(turned[...])
    copies[1].wait()
    first, second = pl.ds(0, part // 2), pl.ds(part // 2, part // 2)
    leaving = [
        pltpu.make_async_copy(wide.at[first], p1, sem.at[4]),
        pltpu.make_async_copy(wide.at[second], p2, sem.at[5]),
        pltpu.make_async_copy(rows, own, sem.at[6]),
    ]
    leaving[0].start()
    leaving[1].start()
    copies[2].wait()
    copies[3].wait()
    leaving[2].start()
    for copy in leaving:
        copy.wait()


def pack(tokens, out_grad, routes, probs, w_gate_up, w_down, n_dp):
    tok, model = tokens.shape
    half = w_down.shape[1]
    part = model // n_dp
    piece = jax.ShapeDtypeStruct((part // 2, 3 * half), bf16)
    anywhere, inside = pl.BlockSpec(memory_space=pl.ANY), pl.BlockSpec(memory_space=pltpu.VMEM)
    return pl.pallas_call(
        functools.partial(pack_kernel, n_dp),
        out_shape=[piece, piece, jax.ShapeDtypeStruct((tok, 2 * model + lanes), bf16)],
        in_specs=[anywhere, anywhere, inside, inside, anywhere, anywhere],
        out_specs=[anywhere] * 3,
        scratch_shapes=[
            pltpu.VMEM((part, 3 * half), bf16),
            pltpu.VMEM((half, part), bf16),
            pltpu.VMEM((tok, 2 * model + lanes), bf16),
            pltpu.SemaphoreType.DMA((7,)),
        ],
        compiler_params=pltpu.CompilerParams(vmem_limit_bytes=56 * 2**20),
        cost_estimate=pl.CostEstimate(flops=1000, bytes_accessed=1000, transcendentals=0),
    )(tokens, out_grad, routes.T, probs.T, w_gate_up, w_down)


def adam_kernel(n_dp, cut, lead_ref, *refs):
    grads = refs[: 2 * n_dp]
    m_ref, v_ref, w_ref, m_out, v_out, w_out = refs[2 * n_dp :]
    upper = pl.program_id(0) < cut
    me_dp = lax.axis_index("dp")
    width = grads[0].shape[1]
    is_lead = lead_ref[0] == me_dp
    for k in range(n_dp):
        grad = jnp.where(upper, grads[2 * k][...].astype(f32), grads[2 * k + 1][...].astype(f32))
        at = lax.rem(me_dp + k, n_dp) * width
        at = pl.ds(pl.multiple_of(at, width), width)
        m_old, v_old = m_ref[0, 0, :, at], v_ref[0, 0, :, at]
        m_new, v_new, w_new = adam_update(grad, m_old, v_old, w_ref[0, :, at])
        m_out[0, 0, :, at] = jnp.where(is_lead, m_new, m_old)
        v_out[0, 0, :, at] = jnp.where(is_lead, v_new, v_old)
        w_out[:, at] = w_new


def adam_call(parts, leader, moment_one, moment_two, w_down):
    half, model = w_down.shape[1:]
    step = math.gcd(64, math.gcd(*[part.shape[0] for part in parts[0]]))
    steps, cut = half // step, parts[0][0].shape[0] // step
    n_dp = len(parts)
    width = model // n_dp
    wide = pl.BlockSpec((1, 1, step, model), lambda i: (0, 0, i, 0))
    return pl.pallas_call(
        functools.partial(adam_kernel, n_dp, cut),
        grid=(steps,),
        out_shape=[
            jax.ShapeDtypeStruct(moment_one.shape, f32),
            jax.ShapeDtypeStruct(moment_two.shape, f32),
            jax.ShapeDtypeStruct((half, model), bf16),
        ],
        in_specs=[pl.BlockSpec(memory_space=pltpu.SMEM)]
        + [
            pl.BlockSpec((step, width), lambda i: (jnp.minimum(i, cut - 1), 0)),
            pl.BlockSpec((step, width), lambda i: (jnp.maximum(i - cut, 0), 0)),
        ]
        * n_dp
        + [wide, wide, pl.BlockSpec((1, step, model), lambda i: (0, i, 0))],
        out_specs=[wide, wide, pl.BlockSpec((step, model), lambda i: (i, 0))],
        compiler_params=pltpu.CompilerParams(vmem_limit_bytes=32 * 2**20),
        cost_estimate=pl.CostEstimate(
            flops=1000, bytes_accessed=1000, transcendentals=0
        ),
    )(leader, *[v for pair in parts for v in pair], moment_one, moment_two, w_down)


def body(
    tokens, out_grad, routes, probs, w_gate_up, w_down, moment_one, moment_two, replicas, leader
):
    tok_dev, model = tokens.shape
    half = w_down.shape[1]
    n_dp = lax.axis_size("dp")
    n_ex = lax.axis_size("expert")
    layers = n_ex // plane
    width = model // n_dp
    me_dp = lax.axis_index("dp")
    def others(value):
        return [turn(value, k) for k in range(1, n_dp)]

    p1, p2, own = pack(tokens, out_grad, routes, probs, w_gate_up, w_down, n_dp)
    w_gu, w_dn = w_gate_up[0], after(w_down, own)[0]
    w_own = jnp.concatenate([w_gu, w_dn.T], 1)
    held = [own, along(own)]
    x_p1, y_p2, x_p2, y_p1 = hop(p1, 1), hop(p2, 2), hop(p2, 1), hop(p1, 2)

    weights = {"w0": w_own}
    make = functools.partial(Pass, tok_dev, model, half, n_dp)
    last_block = layers - 1
    near = list(range(last_block))

    def pick(p):
        got = {"t%d" % k: held[k] for k in p.blocks}
        return got | {k: v for k, v in weights.items() if int(k[1]) in p.slots}

    def name_parts(s, firsts, seconds):
        for k in range(n_dp):
            weights["w%d_%d_0" % (s, k)] = firsts[k]
            weights["w%d_%d_1" % (s, k)] = seconds[k]

    held, w_own, x_p1, y_p2 = lax.optimization_barrier((held, w_own, x_p1, y_p2))
    x_o1, y_o2 = others(x_p1), others(y_p2)
    weights["w0"] = w_own
    zero_pass = make([0], near[:2], [(0, 2)])
    zero = zero_pass.call(pick(zero_pass))
    while len(held) < layers - 1:
        held.append(along(held[-1]))

    x_p1, y_p2, x_p2, y_p1, x_o1, y_o2, held, zero = lax.optimization_barrier(
        (x_p1, y_p2, x_p2, y_p1, x_o1, y_o2, held, zero)
    )
    d_p2, d_p1 = hop(y_p2, 1), hop(x_p1, 2)
    final = along(held[-1])
    x_o2, y_o1 = others(x_p2), others(y_p1)
    name_parts(1, [x_p1] + x_o1, [x_p2] + x_o2)
    name_parts(2, [y_p1] + y_o1, [y_p2] + y_o2)
    one_pass = make([0, 1, 2], near, [(2, last_block)] + [(0, last_block)] * 2)
    one = one_pass.call(pick(one_pass), sums=[(zero_pass, zero)], grads=[(zero, (0, 1))])

    one, d_p1, d_p2, held, final = lax.optimization_barrier((one, d_p1, d_p2, held, final))
    held.append(final)
    d_o1, d_o2 = others(d_p1), others(d_p2)
    name_parts(3, [d_p1] + d_o1, [d_p2] + d_o2)
    two_pass = make([0, 1, 2], [last_block], [(0, 1)] * 3)
    two = two_pass.call(pick(two_pass), grads=[(one, (0, 3))])
    two_send = after(two["send"], d_o1, d_o2)
    swapped = [turn(two_send[:, k - 1], k) for k in range(1, n_dp)]
    keep = two["keep"]

    sums = [(one_pass, one), (two_pass, two)]
    early = near[1:]
    first_pass = make([3], early, [(0, len(early))], len(early))
    first = first_pass.call(pick(first_pass), sums=sums)
    first, swapped, keep = lax.optimization_barrier((first, swapped, keep))
    passing = along(first["back0"])
    cut = half // 2
    top, low = slice(0, cut), slice(cut, half)

    def summed(s, r, keep, swapped):
        return keep[s][r] + sum(v[s][r].astype(f32) for v in swapped)

    sent = [
        hop(summed(1, top, keep, swapped).astype(bf16), 1),
        hop(summed(2, low, keep, swapped).astype(bf16), 2),
    ]
    rest_pass = make([3], [0, last_block], [(0, 2)], 2)
    last = rest_pass.call(pick(rest_pass), sums=sums, grads=[(first, (0, 1))])
    sent, passing, last_keep, last_send, keep, swapped = lax.optimization_barrier(
        (sent, passing, last["keep"], last["send"], keep, swapped)
    )

    across = last_keep[0]
    for k in range(1, n_dp):
        across = across + turn(last_send[0, k - 1], k).astype(f32)
    across = across.astype(bf16)
    came = [hop(across[top], 1), hop(across[low], 2)]
    late = None
    for k in range(2, layers):
        term = first["back%d" % (k - 1)] if k < last_block else last["back1"]
        if k == last_block:
            came, passing = lax.optimization_barrier((came, passing))
            late = [
                (summed(2, top, keep, swapped) + came[0].astype(f32)).astype(bf16),
                (summed(1, low, keep, swapped) + came[1].astype(f32)).astype(bf16),
            ]
        passing = (passing.astype(f32) + term.astype(f32)).astype(bf16)
        late, passing = lax.optimization_barrier((late, passing))
        passing = along(passing)
    late = [hop(late[0], 2), hop(late[1], 1)]

    grads = []
    for r, one_hop, two_hops in zip((top, low), sent, late):
        grad = summed(0, r, keep, swapped) + one_hop.astype(f32) + two_hops.astype(f32)
        grads.append(grad.astype(bf16))
    halves = [others(grad) for grad in grads]
    halves, passing = lax.optimization_barrier((halves, passing))
    parts = [tuple(grads)] + list(zip(*halves))
    new_one, new_two, w_new = adam_call(parts, leader, moment_one, moment_two, w_down)
    lead = leader[0]
    fresh = w_new
    for k in range(1, n_dp):
        fresh = jnp.where((me_dp + k) % n_dp == lead, turn(w_new, k), fresh)

    total = last["back0"].astype(f32) + passing.astype(f32)
    token_grad = total[:, :model].astype(bf16)
    pair = total[:, model:]
    chosen = routes[:, :, None] == jnp.arange(lanes, dtype=jnp.int32)[None, None, :]
    prob_grad = jnp.sum(jnp.where(chosen, pair[:, None, :], 0.0), axis=2).astype(bf16)
    is_live = replicas[0][me_dp] == 1
    new_down = jnp.where(is_live, fresh, w_dn)[None, None]
    return (token_grad, prob_grad, new_down, new_one, new_two)


def solution(mesh):
    in_specs = (
        P(("dp", "expert"), None),
        P(("dp", "expert"), None),
        P(("dp", "expert"), None),
        P(("dp", "expert"), None),
        P("expert", None, None),
        P("expert", None, None),
        P("dp", "expert", None, None),
        P("dp", "expert", None, None),
        P("expert", None),
        P("expert"),
    )
    out_specs = (
        P(("dp", "expert"), None),
        P(("dp", "expert"), None),
        P("dp", "expert", None, None),
        P("dp", "expert", None, None),
        P("dp", "expert", None, None),
    )
    return jax.shard_map(body, mesh=mesh, in_specs=in_specs, out_specs=out_specs, check_vma=False)
```

```python
import functools
import math
import jax
import jax.numpy as jnp
from jax import lax
from jax.experimental import pallas as pl
from jax.experimental.pallas import tpu as pltpu
from jax.sharding import PartitionSpec as P

learn_rate = 0.01
beta_one = 0.9
beta_two = 0.95
adam_eps = 1e-08
weight_decay = 0.1
adam_step = 100

f32 = jnp.float32
bf16 = jnp.bfloat16
plane = 4
lanes = 128
tile = 256


def adam_update(grad, m_old, v_old, w_old):
    m_new = beta_one * m_old + (1.0 - beta_one) * grad
    v_new = beta_two * v_old + (1.0 - beta_two) * grad * grad
    m_hat = m_new / (1.0 - beta_one**adam_step)
    v_hat = v_new / (1.0 - beta_two**adam_step)
    w_wide = w_old.astype(f32)
    w_new = (
        w_wide - learn_rate * (m_hat / (jnp.sqrt(v_hat) + adam_eps) + weight_decay * w_wide)
    ).astype(bf16)
    return (m_new, v_new, w_new)


def hop(value, flip):
    n = lax.axis_size("expert")
    return lax.ppermute(value, "expert", [(i, i ^ flip) for i in range(n)])


def ring(layers):
    return [z for z in range(layers) if z == 0 or z % 2] + [
        z for z in range(layers - 1, 0, -1) if z % 2 == 0
    ]


def along(value):
    n = lax.axis_size("expert")
    order = ring(n // plane)
    pairs = [
        (z * plane + j, order[(r + 1) % len(order)] * plane + j)
        for r, z in enumerate(order)
        for j in range(plane)
    ]
    return lax.ppermute(value, "expert", pairs)


def turn(value, step):
    n = lax.axis_size("dp")
    return lax.ppermute(value, "dp", [((r + step) % n, r) for r in range(n)])


def after(value, *earlier):
    return lax.optimization_barrier((value, *earlier))[0]


def nt(a, b):
    return lax.dot_general(a, b, (((1,), (1,)), ((), ())), preferred_element_type=f32)


def tn(a, b):
    return lax.dot_general(a, b, (((0,), (0,)), ((), ())), preferred_element_type=f32)


class Pass:
    def __init__(self, tok, model, half, n_dp, slots, blocks, spans, back=0):
        self.tok, self.model, self.half, self.n_dp = tok, model, half, n_dp
        self.slots, self.blocks, self.spans, self.back = slots, blocks, spans, back
        self.left = blocks[back:]
        self.rows = tok * len(blocks)
        self.width = model // n_dp

    def kernel(self, n_in, *refs):
        tok, model, half, rows, width = self.tok, self.model, self.half, self.rows, self.width
        n_dp, slots, blocks = self.n_dp, self.slots, self.blocks
        ins = dict(zip(self.names, refs[:n_in]))
        n_out = len(self.outs)
        outs = dict(zip(self.outs, refs[n_in : n_in + n_out]))
        scratch = list(refs[n_in + n_out :])
        xs, ys, ps, ws, gu, hs, pre, sc, dx, pr, keep, send = scratch[:12]
        sem_t, sem_w, sem_i, sem_k, sem_o = scratch[12:17]
        me_dp = lax.axis_index("dp")
        me = lax.axis_index("expert")
        here, layer = lax.rem(me, plane), lax.div(me, plane)

        def row_copies(b):
            ref, at = ins["t%d" % blocks[b]], pl.ds(b * tok, tok)
            first, second = pl.ds(0, model), pl.ds(model, model)
            return (
                pltpu.make_async_copy(ref.at[:, first], xs.at[at], sem_t.at[b, 0]),
                pltpu.make_async_copy(ref.at[:, second], ys.at[at], sem_t.at[b, 1]),
                pltpu.make_async_copy(
                    ref.at[:, pl.ds(2 * model, lanes)], ps.at[at], sem_t.at[b, 2]
                ),
            )

        def weight_copies(i):
            s = slots[i]
            if s == 0:
                return [pltpu.make_async_copy(ins["w0"], ws.at[i % 2], sem_w.at[i, 0])]
            out = []
            for k in range(n_dp):
                for h in range(2):
                    at = lax.rem(me_dp + k, n_dp) * width + h * (width // 2)
                    at = pl.multiple_of(at, width // 2)
                    out.append(
                        pltpu.make_async_copy(
                            ins["w%d_%d_%d" % (s, k, h)],
                            ws.at[i % 2, pl.ds(at, width // 2)],
                            sem_w.at[i, 2 * k + h],
                        )
                    )
            return out

        for b in range(len(blocks)):
            for copy in row_copies(b):
                copy.start()
        for copy in weight_copies(0):
            copy.start()
        extra = []
        for b, place in enumerate(self.sums):
            at = pl.ds(b * tok, tok)
            if place is None:
                dx[at, :] = jnp.zeros((tok, model), f32)
                pr[at, :] = jnp.zeros((tok, lanes), f32)
                continue
            j, row = place
            came = pl.ds(row * tok, tok)
            extra.append(
                pltpu.make_async_copy(ins["dx%d" % j].at[came], dx.at[at], sem_i.at[b, 0])
            )
            extra.append(
                pltpu.make_async_copy(ins["pr%d" % j].at[came], pr.at[at], sem_i.at[b, 1])
            )
        filled = 0
        for j, (low, n) in enumerate(self.grads):
            at, came = pl.ds(filled, n), pl.ds(low, n)
            for name, ref, sem in (("keep", keep, 0), ("send", send, 1)):
                ref_in = ins["%s%d" % (name, j)].at[came]
                extra.append(pltpu.make_async_copy(ref_in, ref.at[at], sem_k.at[j, sem]))
            filled += n
        for copy in extra:
            copy.start()

        for b in range(len(blocks)):
            for copy in row_copies(b):
                copy.wait()
        chunk = min(128, tok)
        lane = lax.broadcasted_iota(jnp.int32, (chunk, lanes), 1)
        pending = []

        for i, s in enumerate(slots):
            for copy in weight_copies(i):
                copy.wait()
            if i + 1 < len(slots):
                for copy in weight_copies(i + 1):
                    copy.start()
            w = ws.at[i % 2]
            low, high = (tok * b for b in self.spans[i])
            mine = slice(low, high)
            for n in range(0, 2 * half, tile):
                gu[mine, n : n + tile] = jnp.dot(
                    xs[mine, :], w[:, n : n + tile], preferred_element_type=f32
                )
            hs[mine, :] = jnp.dot(ys[mine, :], w[:, 2 * half :], preferred_element_type=f32)
            if i == 0:
                for copy in extra:
                    copy.wait()
            expert = layer * plane + lax.bitwise_xor(here, jnp.int32(s))

            @pl.loop(low // chunk, high // chunk)
            def _(r):
                at = pl.ds(pl.multiple_of(r * chunk, chunk), chunk)
                gate, upper, h = gu[at, :half], gu[at, half:], hs[at, :]
                hit = lane == expert
                p = jnp.sum(jnp.where(hit, ps[at, :].astype(f32), 0.0), axis=1, keepdims=True)
                sigma = jax.nn.sigmoid(gate)
                silu = gate * sigma
                hidden = (silu * upper).astype(bf16).astype(f32)
                pair = jnp.sum(hidden * h, axis=1, keepdims=True)
                pr[at, :] += jnp.where(hit, pair, 0.0)
                grad = p * h
                pre[at, :half] = (grad * upper * (sigma * (1.0 + gate * (1.0 - sigma)))).astype(bf16)
                pre[at, half:] = (grad * silu).astype(bf16)
                sc[at, :] = (p * hidden).astype(bf16)

            for d in range(0, model, 2 * tile):
                at = slice(d, d + 2 * tile)
                dx[mine, at] = dx[mine, at] + nt(pre[mine, :], w[at, : 2 * half])
            for d in range(0, width, 2 * tile):
                at = slice(d, d + 2 * tile)
                col = pl.ds(pl.multiple_of(me_dp * width + d, tile), 2 * tile)
                part = tn(sc[mine, :], ys[mine, col])
                keep[i, :, at] = keep[i, :, at] + part if i < filled else part
                for k in range(1, n_dp):
                    col = lax.rem(me_dp + n_dp - k, n_dp) * width + d
                    col = pl.ds(pl.multiple_of(col, tile), 2 * tile)
                    part = tn(sc[mine, :], ys[mine, col])
                    if i < filled:
                        part = send[i, k - 1, :, at].astype(f32) + part
                    send[i, k - 1, :, at] = part.astype(bf16)

            pending.append(
                pltpu.make_async_copy(keep.at[i], outs["keep"].at[i], sem_o.at[2 * i])
            )
            pending.append(
                pltpu.make_async_copy(send.at[i], outs["send"].at[i], sem_o.at[2 * i + 1])
            )
            pending[-2].start()
            pending[-1].start()
        n = 2 * len(slots)
        if self.left:
            at = pl.ds(self.back * tok, len(self.left) * tok)
            pending.append(pltpu.make_async_copy(dx.at[at], outs["dx"], sem_o.at[n]))
            pending.append(pltpu.make_async_copy(pr.at[at], outs["pr"], sem_o.at[n + 1]))
            pending[-2].start()
            pending[-1].start()
        for b in range(self.back):
            rows_out = scratch[17]
            at = pl.ds(b * tok, tok)
            rows_out[b, :, pl.ds(0, model)] = dx[at, :].astype(bf16)
            rows_out[b, :, pl.ds(model, lanes)] = pr[at, :].astype(bf16)
            copy = pltpu.make_async_copy(rows_out.at[b], outs["back%d" % b], sem_o.at[n + 2 + b])
            copy.start()
            pending.append(copy)
        for copy in pending:
            copy.wait()

    def call(self, ins, sums=(), grads=()):
        tok, model, half, rows, width = self.tok, self.model, self.half, self.rows, self.width
        n_dp, n = self.n_dp, len(self.slots)
        ins = dict(ins)
        self.sums = [None] * len(self.blocks)
        for j, (earlier, out) in enumerate(sums):
            for b, block in enumerate(self.blocks):
                if block in earlier.left:
                    self.sums[b] = (j, earlier.left.index(block))
            ins["dx%d" % j], ins["pr%d" % j] = out["dx"], out["pr"]
        self.grads = [rows_from for _, rows_from in grads]
        for j, (out, _) in enumerate(grads):
            ins["keep%d" % j], ins["send%d" % j] = out["keep"], out["send"]
        shape = {"keep": ((n, half, width), f32)}
        shape["send"] = ((n, max(n_dp - 1, 1), half, width), bf16)
        out_rows = (self.back, tok, model + lanes)
        if self.back:
            for b in range(self.back):
                shape["back%d" % b] = (out_rows[1:], bf16)
        if self.left:
            shape["dx"] = ((len(self.left) * tok, model), f32)
            shape["pr"] = ((len(self.left) * tok, lanes), f32)
        self.names, self.outs = list(ins), list(shape)
        scratch = [
            pltpu.VMEM((rows, model), bf16),
            pltpu.VMEM((rows, model), bf16),
            pltpu.VMEM((rows, lanes), bf16),
            pltpu.VMEM((min(n, 2), model, 3 * half), bf16),
            pltpu.VMEM((rows, 2 * half), f32),
            pltpu.VMEM((rows, half), f32),
            pltpu.VMEM((rows, 2 * half), bf16),
            pltpu.VMEM((rows, half), bf16),
            pltpu.VMEM((rows, model), f32),
            pltpu.VMEM((rows, lanes), f32),
            pltpu.VMEM((n, half, width), f32),
            pltpu.VMEM((n, max(n_dp - 1, 1), half, width), bf16),
            pltpu.SemaphoreType.DMA((len(self.blocks), 3)),
            pltpu.SemaphoreType.DMA((n, 2 * n_dp)),
            pltpu.SemaphoreType.DMA((len(self.blocks), 2)),
            pltpu.SemaphoreType.DMA((max(len(self.grads), 1), 2)),
            pltpu.SemaphoreType.DMA((2 * n + len(self.blocks) + 2,)),
        ]
        if self.back:
            scratch.append(pltpu.VMEM(out_rows, bf16))
        out = pl.pallas_call(
            functools.partial(self.kernel, len(ins)),
            out_shape=[jax.ShapeDtypeStruct(*v) for v in shape.values()],
            in_specs=[pl.BlockSpec(memory_space=pl.ANY)] * len(ins),
            out_specs=[pl.BlockSpec(memory_space=pl.ANY)] * len(shape),
            scratch_shapes=scratch,
            compiler_params=pltpu.CompilerParams(vmem_limit_bytes=56 * 2**20),
            cost_estimate=pl.CostEstimate(flops=1000, bytes_accessed=1000, transcendentals=0),
        )(*ins.values())
        return dict(zip(shape, out))


def pack_kernel(n_dp, x_ref, y_ref, routes, probs, gu_ref, dn_ref, p1, p2, own, *scratch):
    wide, turned, rows, sem = scratch
    tok, model = x_ref.shape
    part, half = wide.shape[0], turned.shape[0]
    at = pl.ds(pl.multiple_of(lax.axis_index("dp") * part, part), part)
    copies = [
        pltpu.make_async_copy(dn_ref.at[0, :, at], turned, sem.at[0]),
        pltpu.make_async_copy(gu_ref.at[0, at], wide.at[:, pl.ds(0, 2 * half)], sem.at[1]),
        pltpu.make_async_copy(x_ref, rows.at[:, pl.ds(0, model)], sem.at[2]),
        pltpu.make_async_copy(y_ref, rows.at[:, pl.ds(model, model)], sem.at[3]),
    ]
    for copy in copies:
        copy.start()
    expert = lax.broadcasted_iota(jnp.int32, (lanes, tok), 0)
    named = jnp.zeros((lanes, tok), f32)
    p = probs[...].astype(f32)
    for k in range(routes.shape[0]):
        named = named + jnp.where(expert == routes[k : k + 1, :], p[k : k + 1, :], 0.0)
    rows[:, 2 * model :] = jnp.transpose(named).astype(bf16)
    copies[0].wait()
    wide[:, 2 * half :] = jnp.transpose(turned[...])
    copies[1].wait()
    first, second = pl.ds(0, part // 2), pl.ds(part // 2, part // 2)
    leaving = [
        pltpu.make_async_copy(wide.at[first], p1, sem.at[4]),
        pltpu.make_async_copy(wide.at[second], p2, sem.at[5]),
        pltpu.make_async_copy(rows, own, sem.at[6]),
    ]
    leaving[0].start()
    leaving[1].start()
    copies[2].wait()
    copies[3].wait()
    leaving[2].start()
    for copy in leaving:
        copy.wait()


def pack(tokens, out_grad, routes, probs, w_gate_up, w_down, n_dp):
    tok, model = tokens.shape
    half = w_down.shape[1]
    part = model // n_dp
    piece = jax.ShapeDtypeStruct((part // 2, 3 * half), bf16)
    anywhere, inside = pl.BlockSpec(memory_space=pl.ANY), pl.BlockSpec(memory_space=pltpu.VMEM)
    return pl.pallas_call(
        functools.partial(pack_kernel, n_dp),
        out_shape=[piece, piece, jax.ShapeDtypeStruct((tok, 2 * model + lanes), bf16)],
        in_specs=[anywhere, anywhere, inside, inside, anywhere, anywhere],
        out_specs=[anywhere] * 3,
        scratch_shapes=[
            pltpu.VMEM((part, 3 * half), bf16),
            pltpu.VMEM((half, part), bf16),
            pltpu.VMEM((tok, 2 * model + lanes), bf16),
            pltpu.SemaphoreType.DMA((7,)),
        ],
        compiler_params=pltpu.CompilerParams(vmem_limit_bytes=56 * 2**20),
        cost_estimate=pl.CostEstimate(flops=1000, bytes_accessed=1000, transcendentals=0),
    )(tokens, out_grad, routes.T, probs.T, w_gate_up, w_down)


def adam_kernel(n_dp, cut, lead_ref, *refs):
    grads = refs[: 2 * n_dp]
    m_ref, v_ref, w_ref, m_out, v_out, w_out = refs[2 * n_dp :]
    upper = pl.program_id(0) < cut
    me_dp = lax.axis_index("dp")
    width = grads[0].shape[1]
    is_lead = lead_ref[0] == me_dp
    for k in range(n_dp):
        grad = jnp.where(upper, grads[2 * k][...].astype(f32), grads[2 * k + 1][...].astype(f32))
        at = lax.rem(me_dp + k, n_dp) * width
        at = pl.ds(pl.multiple_of(at, width), width)
        m_old, v_old = m_ref[0, 0, :, at], v_ref[0, 0, :, at]
        m_new, v_new, w_new = adam_update(grad, m_old, v_old, w_ref[0, :, at])
        m_out[0, 0, :, at] = jnp.where(is_lead, m_new, m_old)
        v_out[0, 0, :, at] = jnp.where(is_lead, v_new, v_old)
        w_out[:, at] = w_new


def adam_call(parts, leader, moment_one, moment_two, w_down):
    half, model = w_down.shape[1:]
    step = math.gcd(64, math.gcd(*[part.shape[0] for part in parts[0]]))
    steps, cut = half // step, parts[0][0].shape[0] // step
    n_dp = len(parts)
    width = model // n_dp
    wide = pl.BlockSpec((1, 1, step, model), lambda i: (0, 0, i, 0))
    return pl.pallas_call(
        functools.partial(adam_kernel, n_dp, cut),
        grid=(steps,),
        out_shape=[
            jax.ShapeDtypeStruct(moment_one.shape, f32),
            jax.ShapeDtypeStruct(moment_two.shape, f32),
            jax.ShapeDtypeStruct((half, model), bf16),
        ],
        in_specs=[pl.BlockSpec(memory_space=pltpu.SMEM)]
        + [
            pl.BlockSpec((step, width), lambda i: (jnp.minimum(i, cut - 1), 0)),
            pl.BlockSpec((step, width), lambda i: (jnp.maximum(i - cut, 0), 0)),
        ]
        * n_dp
        + [wide, wide, pl.BlockSpec((1, step, model), lambda i: (0, i, 0))],
        out_specs=[wide, wide, pl.BlockSpec((step, model), lambda i: (i, 0))],
        compiler_params=pltpu.CompilerParams(vmem_limit_bytes=12 * 2**20),
        cost_estimate=pl.CostEstimate(
            flops=1000, bytes_accessed=1000, transcendentals=0
        ),
    )(leader, *[v for pair in parts for v in pair], moment_one, moment_two, w_down)


def body(
    tokens, out_grad, routes, probs, w_gate_up, w_down, moment_one, moment_two, replicas, leader
):
    tok_dev, model = tokens.shape
    half = w_down.shape[1]
    n_dp = lax.axis_size("dp")
    n_ex = lax.axis_size("expert")
    layers = n_ex // plane
    width = model // n_dp
    me_dp = lax.axis_index("dp")
    def others(value):
        return [turn(value, k) for k in range(1, n_dp)]

    p1, p2, own = pack(tokens, out_grad, routes, probs, w_gate_up, w_down, n_dp)
    w_gu, w_dn = w_gate_up[0], after(w_down, own)[0]
    w_own = jnp.concatenate([w_gu, w_dn.T], 1)
    held = [own, along(own)]
    x_p1, y_p2, x_p2, y_p1 = hop(p1, 1), hop(p2, 2), hop(p2, 1), hop(p1, 2)

    weights = {"w0": w_own}
    make = functools.partial(Pass, tok_dev, model, half, n_dp)
    last_block = layers - 1
    near = list(range(last_block))

    def pick(p):
        got = {"t%d" % k: held[k] for k in p.blocks}
        return got | {k: v for k, v in weights.items() if int(k[1]) in p.slots}

    def name_parts(s, firsts, seconds):
        for k in range(n_dp):
            weights["w%d_%d_0" % (s, k)] = firsts[k]
            weights["w%d_%d_1" % (s, k)] = seconds[k]

    held, w_own, x_p1, y_p2 = lax.optimization_barrier((held, w_own, x_p1, y_p2))
    x_o1, y_o2 = others(x_p1), others(y_p2)
    weights["w0"] = w_own
    zero_pass = make([0], near[:2], [(0, 2)])
    zero = zero_pass.call(pick(zero_pass))
    while len(held) < layers - 1:
        held.append(along(held[-1]))

    x_p1, y_p2, x_p2, y_p1, x_o1, y_o2, held, zero = lax.optimization_barrier(
        (x_p1, y_p2, x_p2, y_p1, x_o1, y_o2, held, zero)
    )
    d_p2, d_p1 = hop(y_p2, 1), hop(x_p1, 2)
    final = along(held[-1])
    x_o2, y_o1 = others(x_p2), others(y_p1)
    name_parts(1, [x_p1] + x_o1, [x_p2] + x_o2)
    name_parts(2, [y_p1] + y_o1, [y_p2] + y_o2)
    one_pass = make([0, 1, 2], near, [(2, last_block)] + [(0, last_block)] * 2)
    one = one_pass.call(pick(one_pass), sums=[(zero_pass, zero)], grads=[(zero, (0, 1))])

    one, d_p1, d_p2, held, final = lax.optimization_barrier((one, d_p1, d_p2, held, final))
    held.append(final)
    d_o1, d_o2 = others(d_p1), others(d_p2)
    name_parts(3, [d_p1] + d_o1, [d_p2] + d_o2)
    two_pass = make([0, 1, 2], [last_block], [(0, 1)] * 3)
    two = two_pass.call(pick(two_pass), grads=[(one, (0, 3))])
    two_send = after(two["send"], d_o1, d_o2)
    swapped = [turn(two_send[:, k - 1], k) for k in range(1, n_dp)]
    keep = two["keep"]

    sums = [(one_pass, one), (two_pass, two)]
    early = near[1:]
    first_pass = make([3], early, [(0, len(early))], len(early))
    first = first_pass.call(pick(first_pass), sums=sums)
    first, swapped, keep = lax.optimization_barrier((first, swapped, keep))
    passing = along(first["back0"])
    cut = half // 2
    top, low = slice(0, cut), slice(cut, half)

    def summed(s, r, keep, swapped):
        return keep[s][r] + sum(v[s][r].astype(f32) for v in swapped)

    sent = [
        hop(summed(1, top, keep, swapped).astype(bf16), 1),
        hop(summed(2, low, keep, swapped).astype(bf16), 2),
    ]
    rest_pass = make([3], [0, last_block], [(0, 2)], 2)
    last = rest_pass.call(pick(rest_pass), sums=sums, grads=[(first, (0, 1))])
    sent, passing, last_keep, last_send, keep, swapped = lax.optimization_barrier(
        (sent, passing, last["keep"], last["send"], keep, swapped)
    )

    across = last_keep[0]
    for k in range(1, n_dp):
        across = across + turn(last_send[0, k - 1], k).astype(f32)
    across = across.astype(bf16)
    came = [hop(across[top], 1), hop(across[low], 2)]
    late = None
    for k in range(2, layers):
        term = first["back%d" % (k - 1)] if k < last_block else last["back1"]
        if k == last_block:
            came, passing = lax.optimization_barrier((came, passing))
            late = [
                (summed(2, top, keep, swapped) + came[0].astype(f32)).astype(bf16),
                (summed(1, low, keep, swapped) + came[1].astype(f32)).astype(bf16),
            ]
        passing = (passing.astype(f32) + term.astype(f32)).astype(bf16)
        late, passing = lax.optimization_barrier((late, passing))
        passing = along(passing)
    late = [hop(late[0], 2), hop(late[1], 1)]

    grads = []
    for r, one_hop, two_hops in zip((top, low), sent, late):
        grad = summed(0, r, keep, swapped) + one_hop.astype(f32) + two_hops.astype(f32)
        grads.append(grad.astype(bf16))
    halves = [others(grad) for grad in grads]
    halves, passing = lax.optimization_barrier((halves, passing))
    parts = [tuple(grads)] + list(zip(*halves))
    new_one, new_two, w_new = adam_call(parts, leader, moment_one, moment_two, w_down)
    lead = leader[0]
    fresh = w_new
    for k in range(1, n_dp):
        fresh = jnp.where((me_dp + k) % n_dp == lead, turn(w_new, k), fresh)

    total = last["back0"].astype(f32) + passing.astype(f32)
    token_grad = total[:, :model].astype(bf16)
    pair = total[:, model:]
    chosen = routes[:, :, None] == jnp.arange(lanes, dtype=jnp.int32)[None, None, :]
    prob_grad = jnp.sum(jnp.where(chosen, pair[:, None, :], 0.0), axis=2).astype(bf16)
    is_live = replicas[0][me_dp] == 1
    new_down = jnp.where(is_live, fresh, w_dn)[None, None]
    return (token_grad, prob_grad, new_down, new_one, new_two)


def solution(mesh):
    in_specs = (
        P(("dp", "expert"), None),
        P(("dp", "expert"), None),
        P(("dp", "expert"), None),
        P(("dp", "expert"), None),
        P("expert", None, None),
        P("expert", None, None),
        P("dp", "expert", None, None),
        P("dp", "expert", None, None),
        P("expert", None),
        P("expert"),
    )
    out_specs = (
        P(("dp", "expert"), None),
        P(("dp", "expert"), None),
        P("dp", "expert", None, None),
        P("dp", "expert", None, None),
        P("dp", "expert", None, None),
    )
    return jax.shard_map(body, mesh=mesh, in_specs=in_specs, out_specs=out_specs, check_vma=False)
```
